256 devices in a mesh: sec: 64 (over x, z, core), op: 4 (over y).
Axes of the slice: x: 4, y: 4, z: 8, core: 2. Of those that a mesh axis runs over, the one named last changes fastest.
Arguments:
- wavefunction: bfloat16 [4096, 128, 128], P('sec')
- vectors: bfloat16 [2, 4096, 128, 128], P(None, 'sec')
- left_env: bfloat16 [16, 1024, 128, 128], P('op', 'sec')
- right_env: bfloat16 [16, 1024, 128, 128], P('op', 'sec')
- left_pattern: int32 [16, 1024], P('op', 'sec'), may hold values 0 or 1
- right_pattern: int32 [16, 1024], P('op', 'sec'), may hold values 0 or 1
- block_left: int32 [4096], P('sec'), may hold values from 0 to 1023, as said below
- block_right: int32 [4096], replicated, may hold values from 0 to 1023, as said below
- left_dims: int32 [1024], P('sec'), may hold values from 32 to 128
- right_dims: int32 [1024], replicated, may hold values from 32 to 128
Outputs:
- sigma: bfloat16 [4096, 128, 128], P('sec', 'op')
- residual: bfloat16 [4096, 128, 128], P('sec', 'op')
- correlations: float32 [2], replicated
The draws below stay inside these ranges and needn't reach their ends.
Inputs may be any that keep to these rules, and one draw needn't show every extreme that they name: Block b has a left sector with block_left[b] // 16 == b // 64. `block_right`: right sector j is owned by the index j // 16 of sec; of the 64 blocks of one index of sec, at most 2 have right sectors of one owner, and some owner has exactly 2 from every index of sec.
All inputs are finite; a program needn't handle non-finite values. No bound on the sum of `left_pattern` or of `right_pattern` on one device may be relied on, other than what follows from the above.
Results may differ from the reference program's by a relative error of at most 0.035.
Values may be sent and summed in bfloat16 or wider, within the bound.
No kernel may reach another device: no remote copies, remote signals or barrier semaphores. Data moves between devices by JAX's collectives and lax.ppermute only.
A program may use at most 192 MiB of HBM per device.

```python
import math
import jax
import jax.numpy as jnp
from jax import lax

BLK = 128
NL = 1024
NR = 1024
NVEC = 2
BLK_DEV = 64
NBLK = 4096
TERMS = 16
N_SEC = 64


def scaled_blocks(base, key_rows, key_cols, rise, factor):
    count = base.shape[-3]
    ramp = rise ** (jnp.arange(count, dtype=jnp.float32) / count)
    rows_scale = jnp.exp(jax.random.uniform(key_rows, (count, base.shape[-2], 1), jnp.float32) * math.log(10.0))
    cols_scale = jnp.exp(jax.random.uniform(key_cols, (count, 1, base.shape[-1]), jnp.float32) * math.log(10.0))
    return base * ramp[:, None, None] * rows_scale * cols_scale * factor


def dominant_env(off_part, key_diag, count):
    diag_scale = jax.random.uniform(key_diag, (TERMS, count, 1, 1), jnp.float32, 0.5, 1.5)
    identity = (jnp.arange(BLK)[:, None] == jnp.arange(BLK)[None, :]).astype(jnp.float32)
    return (off_part / math.sqrt(BLK) + diag_scale * identity).astype(jnp.bfloat16)


def draw_wavefunction(key, part):
    key = jax.random.fold_in(key, 3)
    key_base, key_rows, key_cols = jax.random.split(key, 3)
    base = jax.random.normal(key_base, (NBLK, BLK, BLK), jnp.float32)
    rise = 3.0
    return scaled_blocks(base, key_rows, key_cols, rise, 0.1).astype(jnp.bfloat16)


def draw_vectors(key, part):
    key = jax.random.fold_in(key, 4)
    key_base, key_rows, key_cols = jax.random.split(key, 3)
    factor = 1.0 / (BLK * math.sqrt(NBLK))
    base = jax.random.normal(key_base, (NVEC, NBLK, BLK, BLK), jnp.float32)
    rise = 3.0
    return scaled_blocks(base, key_rows, key_cols, rise, factor * 4.0).astype(jnp.bfloat16)


def draw_left_env(key, part):
    key = jax.random.fold_in(key, 5)
    key_off, key_diag = jax.random.split(key)
    off_part = jax.random.normal(key_off, (TERMS, NL, BLK, BLK), jnp.float32)
    return dominant_env(off_part, key_diag, NL)


def draw_right_env(key, part):
    key = jax.random.fold_in(key, 6)
    key_off, key_diag = jax.random.split(key)
    off_part = jax.random.normal(key_off, (TERMS, NR, BLK, BLK), jnp.float32)
    return dominant_env(off_part, key_diag, NR)


def live_dims(key, count):
    key_dims, key_spot = jax.random.split(key)
    dims = jax.random.randint(key_dims, (count,), BLK // 4, BLK + 1)
    spot = jax.random.randint(key_spot, (), 0, count)
    return dims.at[spot].set(BLK).astype(jnp.int32)


def draw_left_dims(key, part):
    key = jax.random.fold_in(key, 7)
    return live_dims(key, NL)


def draw_right_dims(key, part):
    key = jax.random.fold_in(key, 8)
    return live_dims(key, NR)


def draw_block_left(key, part):
    key = jax.random.fold_in(key, 13)
    device_count = NBLK // BLK_DEV
    per_device = NL // device_count
    local_sector = jax.random.randint(key, (NBLK,), 0, per_device)
    owner = jnp.arange(NBLK, dtype=jnp.int32) // BLK_DEV
    return (owner * per_device + local_sector).astype(jnp.int32)


def draw_block_right(key, part):
    key = jax.random.fold_in(key, 11)
    device_count = NBLK // BLK_DEV
    capacity = 2 * BLK_DEV // device_count
    per_device = NR // device_count
    key_hub, key_spread, key_sector = jax.random.split(key, 3)
    busiest = jax.random.randint(key_hub, (), 0, device_count)
    others = jnp.arange(device_count - 1, dtype=jnp.int32)
    others = jnp.where(others >= busiest, others + 1, others)
    pool = jnp.tile(others, capacity)

    def one_source(source_key):
        key_pick, key_order = jax.random.split(source_key)
        spread = jax.random.permutation(key_pick, pool)[:BLK_DEV - capacity]
        targets = jnp.concatenate([jnp.full((capacity,), busiest, jnp.int32), spread])
        return jax.random.permutation(key_order, targets)
    owners = jax.vmap(one_source)(jax.random.split(key_spread, device_count))
    local_sector = jax.random.randint(key_sector, (device_count, BLK_DEV), 0, per_device)
    return (owners * per_device + local_sector).reshape(NBLK).astype(jnp.int32)


def place_ends(entries, stream_key, smallest, largest):
    spot = [jax.random.randint(jax.random.fold_in(stream_key, axis), (), 0, length) for axis, length in enumerate(entries.shape)]
    main_axis = entries.shape.index(max(entries.shape))
    next_to = spot[:main_axis] + [(spot[main_axis] + 1) % entries.shape[main_axis]] + spot[main_axis + 1:]
    return entries.at[tuple(spot)].set(smallest).at[tuple(next_to)].set(largest)


def setup_inputs(seed: int = 0) -> dict:
    arg_keys = jax.random.split(jax.random.key(seed), 11)
    wavefunction = draw_wavefunction(jax.random.fold_in(arg_keys[10], 71), 0)
    vectors = draw_vectors(jax.random.fold_in(arg_keys[10], 71), 0)
    left_env = draw_left_env(jax.random.fold_in(arg_keys[10], 71), 0)
    right_env = draw_right_env(jax.random.fold_in(arg_keys[10], 71), 0)
    left_pattern = place_ends((jax.random.randint(arg_keys[4], (TERMS, NL), 0, 4) < 3).astype(jnp.int32), jax.random.fold_in(arg_keys[4], 1), 0, 1)
    right_pattern = place_ends((jax.random.randint(arg_keys[5], (TERMS, NR), 0, 4) < 3).astype(jnp.int32), jax.random.fold_in(arg_keys[5], 1), 0, 1)
    block_left = draw_block_left(jax.random.fold_in(arg_keys[10], 71), 0)
    block_right = draw_block_right(jax.random.fold_in(arg_keys[10], 71), 0)
    left_dims = draw_left_dims(jax.random.fold_in(arg_keys[10], 71), 0)
    right_dims = draw_right_dims(jax.random.fold_in(arg_keys[10], 71), 0)
    return dict(wavefunction=wavefunction, vectors=vectors, left_env=left_env, right_env=right_env, left_pattern=left_pattern, right_pattern=right_pattern, block_left=block_left, block_right=block_right, left_dims=left_dims, right_dims=right_dims)


def live_mask(lefts, rights, left_dims, right_dims):
    positions = jnp.arange(BLK, dtype=jnp.int32)
    row_live = positions[None, :] < left_dims[lefts][:, None]
    col_live = positions[None, :] < right_dims[rights][:, None]
    return row_live[:, :, None] & col_live[:, None, :]


def reference(wavefunction, vectors, left_env, right_env, left_pattern, right_pattern, block_left, block_right, left_dims, right_dims):
    def one_group(group_index):
        start = (group_index * BLK_DEV).astype(jnp.int32)
        lefts = lax.dynamic_slice_in_dim(block_left, start, BLK_DEV)
        rights = lax.dynamic_slice_in_dim(block_right, start, BLK_DEV)
        live = live_mask(lefts, rights, left_dims, right_dims)
        raw_blocks = lax.dynamic_slice_in_dim(wavefunction, start, BLK_DEV)
        amplitudes = jnp.where(live, raw_blocks, jnp.zeros_like(raw_blocks)).astype(jnp.float32)
        left_table = left_env[:, lefts].astype(jnp.float32) * left_pattern[:, lefts][:, :, None, None].astype(jnp.float32)
        left_terms = jnp.einsum('tbij,bjk->tbik', left_table, amplitudes).astype(jnp.bfloat16)
        left_terms = lax.optimization_barrier(left_terms).astype(jnp.float32)
        right_table = right_env[:, rights].astype(jnp.float32) * right_pattern[:, rights][:, :, None, None].astype(jnp.float32)
        sigma_full = jnp.einsum('tbik,tblk->bil', left_terms, right_table)
        sigma_full = jnp.where(live, sigma_full, jnp.zeros_like(sigma_full))
        chosen = lax.dynamic_slice_in_dim(vectors, start, BLK_DEV, 1).astype(jnp.float32)
        cross_sum = jnp.sum(amplitudes * sigma_full)
        square_sum = jnp.sum(amplitudes * amplitudes)
        vector_sums = jnp.einsum('vbik,bik->v', chosen, sigma_full)
        return sigma_full, cross_sum, square_sum, vector_sums, amplitudes

    sigma_full, cross_sum, square_sum, vector_sums, amplitudes = lax.map(one_group, jnp.arange(N_SEC, dtype=jnp.int32))
    theta = jnp.sum(cross_sum) / jnp.sum(square_sum)
    sigma_full = sigma_full.reshape(NBLK, BLK, BLK)
    amplitudes = amplitudes.reshape(NBLK, BLK, BLK)
    residual = (sigma_full - theta * amplitudes).astype(jnp.bfloat16)
    return sigma_full.astype(jnp.bfloat16), residual, jnp.sum(vector_sums, axis=0)
```

```python
import jax
import jax.numpy as jnp
from jax import lax
from jax.experimental import pallas as pl
from jax.experimental.pallas import tpu as pltpu
from jax.sharding import PartitionSpec as P

NX, NZ, NC, NY = 4, 8, 2, 4
NG = NX * NC
BLOCKS, WIDTH, TERMS, SECTORS = 64, 128, 4, 16
ROWS = WIDTH // NY
VMEM = 48 * 1024 * 1024


def sec_index(x, z, c):
    return (x * NZ + z) * NC + c


GROUP_XC = [[sec_index(x, z, c) for x in range(NX) for c in range(NC)] for z in range(NZ)]
GROUP_Z = [[sec_index(x, z, c) for z in range(NZ)] for x in range(NX) for c in range(NC)]
RING_UP = [
    (sec_index(x, z, c), sec_index(x, (z + 1) % NZ, c))
    for x in range(NX)
    for z in range(NZ)
    for c in range(NC)
]
RING_DOWN = [(d, s) for s, d in RING_UP]
CHUNKS = ((0, 1, 7), (2, 6), (3, 5), (4,))


def smem():
    return pl.BlockSpec(memory_space=pltpu.SMEM)


def vmem():
    return pl.BlockSpec(memory_space=pltpu.VMEM)


def pack_kernel(place, block_left, block_right, left_dims, right_dims, psi, send, meta, route, rlim, clim, count):
    sec = place[0]
    z_here = place[1]

    def clear(i, carry):
        count[i] = 0
        return carry

    lax.fori_loop(0, NX * NZ * NC, clear, 0)

    def clear_meta(i, carry):
        meta[i] = -1
        return carry

    lax.fori_loop(0, NG * NZ * 2, clear_meta, 0)
    rows = lax.broadcasted_iota(jnp.int32, (WIDTH, WIDTH), 0)
    cols = lax.broadcasted_iota(jnp.int32, (WIDTH, WIDTH), 1)

    def one(b, carry):
        left = block_left[b] - sec * SECTORS
        right = block_right[sec * BLOCKS + b]
        owner = lax.shift_right_logical(right, 4)
        rank = count[owner]
        count[owner] = rank + 1
        x_r = lax.shift_right_logical(owner, 4)
        z_r = lax.shift_right_logical(owner, 1) & 7
        group = x_r * 2 + (owner & 1)
        delta = (z_r - z_here) & 7
        slot = group * 16 + delta * 2 + rank
        meta[slot] = left * 16 + (right & 15)
        route[b] = slot
        rl = left_dims[left]
        cl = right_dims[right]
        rlim[b] = rl
        clim[b] = cl
        block = psi[b].astype(jnp.float32)
        live = (rows < rl) & (cols < cl)
        send[slot] = jnp.where(live, block, 0.0).astype(jnp.bfloat16)
        return carry

    lax.fori_loop(0, BLOCKS, one, 0)


def pack(place, block_left, block_right, left_dims, right_dims, psi):
    slots = NG * NZ * 2
    return pl.pallas_call(
        pack_kernel,
        in_specs=[smem(), smem(), smem(), smem(), smem(), vmem()],
        out_specs=[vmem(), smem(), smem(), smem(), smem()],
        out_shape=[
            jax.ShapeDtypeStruct((slots, WIDTH, WIDTH), jnp.bfloat16),
            jax.ShapeDtypeStruct((slots,), jnp.int32),
            jax.ShapeDtypeStruct((BLOCKS,), jnp.int32),
            jax.ShapeDtypeStruct((BLOCKS,), jnp.int32),
            jax.ShapeDtypeStruct((BLOCKS,), jnp.int32),
        ],
        scratch_shapes=[pltpu.SMEM((NX * NZ * NC,), jnp.int32)],
        compiler_params=pltpu.CompilerParams(vmem_limit_bytes=VMEM),
        cost_estimate=pl.CostEstimate(flops=0, bytes_accessed=24 * 2**20, transcendentals=0),
        name="pack",
    )(place, block_left, block_right, left_dims, right_dims, psi)


def contract(deltas, psi_slots, left_all, rights, meta):
    width = len(deltas)
    steps = NG * width * 2

    def split(i):
        return i // (2 * width), (i // 2) % width, i % 2

    def delta_of(k):
        value = deltas[0]
        for n in range(1, width):
            value = jnp.where(k == n, deltas[n], value)
        return value

    def code(i, meta):
        g, k, r = split(i)
        return meta[g * 16 + delta_of(k) * 2 + r]

    def psi_map(i, meta):
        g, k, r = split(i)
        return (g, delta_of(k), r, 0, 0)

    def left_map(i, meta):
        g, k, r = split(i)
        return (g, 0, lax.shift_right_logical(jnp.maximum(code(i, meta), 0), 4), 0, 0)

    def right_map(n):
        def index(i, meta):
            g, k, r = split(i)
            at = g * 2 * width + n * 2 + jnp.where(k == n, r, jnp.where(k > n, 1, 0))
            return (0, jnp.maximum(code(at, meta), 0) & 15, 0, 0)

        return index

    def out_map(i, meta):
        g, k, r = split(i)
        return (g, k, r, 0, 0)

    def kernel(meta, psi, left, *rest):
        right_refs, out = rest[:-1], rest[-1]
        i = pl.program_id(0)
        g, k, r = split(i)

        def work(low, high):
            amp = psi[0, 0, 0]
            terms = lax.dot_general(
                left[0, :, 0].reshape(TERMS * WIDTH, WIDTH),
                amp,
                (((1,), (0,)), ((), ())),
                preferred_element_type=jnp.float32,
            ).astype(jnp.bfloat16)
            total = None
            for a in range(TERMS):
                ref = low if a < 2 else high
                part = lax.dot_general(
                    terms[a * WIDTH : (a + 1) * WIDTH],
                    ref[a % 2, 0],
                    (((1,), (1,)), ((), ())),
                    preferred_element_type=jnp.float32,
                )
                total = part if total is None else total + part
            out[0, 0, 0] = total

        valid = code(i, meta) >= 0
        for n in range(width):

            @pl.when(valid & (k == n))
            def _():
                work(right_refs[2 * n], right_refs[2 * n + 1])

    right_specs = []
    for n in range(width):
        right_specs += [pl.BlockSpec((2, 1, WIDTH, WIDTH), right_map(n))] * 2
    return pl.pallas_call(
        kernel,
        grid_spec=pltpu.PrefetchScalarGridSpec(
            num_scalar_prefetch=1,
            grid=(steps,),
            in_specs=[
                pl.BlockSpec((1, 1, 1, WIDTH, WIDTH), psi_map),
                pl.BlockSpec((1, TERMS, 1, WIDTH, WIDTH), left_map),
            ]
            + right_specs,
            out_specs=pl.BlockSpec((1, 1, 1, WIDTH, WIDTH), out_map),
        ),
        out_shape=jax.ShapeDtypeStruct((NG, width, 2, WIDTH, WIDTH), jnp.float32),
        compiler_params=pltpu.CompilerParams(vmem_limit_bytes=VMEM),
        cost_estimate=pl.CostEstimate(
            flops=steps * 2 * TERMS * 2 * WIDTH**3, bytes_accessed=steps * 352 * 1024, transcendentals=0
        ),
        name="contract",
    )(meta, psi_slots, left_all, *[half for pair in rights for half in pair])


def finish_kernel(place, route, rlim, clim, psi, vectors, *rest):
    returned, (sigma16, sigma32, sums) = rest[: len(CHUNKS)], rest[len(CHUNKS) :]
    first_row = place[2] * ROWS
    rows = lax.broadcasted_iota(jnp.int32, (ROWS, WIDTH), 0) + first_row
    cols = lax.broadcasted_iota(jnp.int32, (ROWS, WIDTH), 1)

    def one(b, carry):
        cross, square, first, second = carry
        slot = route[b]
        group = lax.shift_right_logical(slot, 4)
        delta = lax.shift_right_logical(slot, 1) & 7
        rank = slot & 1
        for n, deltas in enumerate(CHUNKS):
            for k, d in enumerate(deltas):

                @pl.when(delta == d)
                def _():
                    sigma32[b] = returned[n][group, k, rank]

        live = (rows < rlim[b]) & (cols < clim[b])
        value = jnp.where(live, sigma32[b], 0.0)
        amp = jnp.where(live, psi[b].astype(jnp.float32), 0.0)
        sigma32[b] = value
        sigma16[b] = value.astype(jnp.bfloat16)
        return (
            cross + amp * value,
            square + amp * amp,
            first + vectors[0, b].astype(jnp.float32) * value,
            second + vectors[1, b].astype(jnp.float32) * value,
        )

    zero = jnp.zeros((ROWS, WIDTH), jnp.float32)
    totals = lax.fori_loop(0, BLOCKS, one, (zero, zero, zero, zero))
    for n in range(4):
        sums[n] = jnp.sum(totals[n].reshape(ROWS // 8, 8, WIDTH), axis=0)


def finish(place, route, rlim, clim, psi, vectors, returned):
    def whole(shape):
        return pl.BlockSpec(shape, lambda i, *_: (0,) * len(shape))

    part = (BLOCKS, ROWS, WIDTH)
    return pl.pallas_call(
        finish_kernel,
        grid_spec=pltpu.PrefetchScalarGridSpec(
            num_scalar_prefetch=4,
            grid=(1,),
            in_specs=[
                pl.BlockSpec(part, lambda i, place, *_: (0, place[2], 0)),
                pl.BlockSpec((2,) + part, lambda i, place, *_: (0, 0, place[2], 0)),
            ]
            + [whole(r.shape) for r in returned],
            out_specs=[whole(part), whole(part), whole((4, 8, WIDTH))],
        ),
        out_shape=[
            jax.ShapeDtypeStruct(part, jnp.bfloat16),
            jax.ShapeDtypeStruct(part, jnp.float32),
            jax.ShapeDtypeStruct((4, 8, WIDTH), jnp.float32),
        ],
        compiler_params=pltpu.CompilerParams(vmem_limit_bytes=VMEM),
        cost_estimate=pl.CostEstimate(flops=0, bytes_accessed=10 * 2**20, transcendentals=0),
        name="finish",
    )(place, route, rlim, clim, psi, vectors, *returned)


def residual_kernel(place, rlim, clim, psi, sigma32, theta, out):
    first_row = place[2] * ROWS
    rows = lax.broadcasted_iota(jnp.int32, (ROWS, WIDTH), 0) + first_row
    cols = lax.broadcasted_iota(jnp.int32, (ROWS, WIDTH), 1)
    scale = theta[...]

    def one(b, carry):
        live = (rows < rlim[b]) & (cols < clim[b])
        amp = jnp.where(live, psi[b].astype(jnp.float32), 0.0)
        out[b] = (sigma32[b] - scale * amp).astype(jnp.bfloat16)
        return carry

    lax.fori_loop(0, BLOCKS, one, 0)


def make_residual(place, rlim, clim, psi, sigma32, theta):
    part = (BLOCKS, ROWS, WIDTH)
    return pl.pallas_call(
        residual_kernel,
        grid_spec=pltpu.PrefetchScalarGridSpec(
            num_scalar_prefetch=3,
            grid=(1,),
            in_specs=[
                pl.BlockSpec(part, lambda i, place, *_: (0, place[2], 0)),
                pl.BlockSpec(part, lambda i, *_: (0, 0, 0)),
                pl.BlockSpec((1, WIDTH), lambda i, *_: (0, 0)),
            ],
            out_specs=pl.BlockSpec(part, lambda i, *_: (0, 0, 0)),
        ),
        out_shape=jax.ShapeDtypeStruct(part, jnp.bfloat16),
        compiler_params=pltpu.CompilerParams(vmem_limit_bytes=VMEM),
        name="residual",
    )(place, rlim, clim, psi, sigma32, theta)


def exchange_groups(x):
    return lax.all_to_all(x, "sec", 0, 0, axis_index_groups=GROUP_XC)


def body(
    wavefunction,
    vectors,
    left_env,
    right_env,
    left_pattern,
    right_pattern,
    block_left,
    block_right,
    left_dims,
    right_dims,
):
    sec = lax.axis_index("sec").astype(jnp.int32)
    op = lax.axis_index("op").astype(jnp.int32)
    place = jnp.stack([sec, (sec // NC) % NZ, op]).astype(jnp.int32)

    right_table = right_env * right_pattern[:, :, None, None].astype(jnp.bfloat16)
    left_table = left_env * left_pattern[:, :, None, None].astype(jnp.bfloat16)
    halves = (right_table[:2], right_table[2:])
    rights = {0: halves}
    up, down = halves, halves
    for step in range(1, 4):
        up = tuple(lax.ppermute(h, "sec", RING_UP) for h in up)
        down = tuple(lax.ppermute(h, "sec", RING_DOWN) for h in down)
        rights[NZ - step] = up
        rights[step] = down
    rights[4] = (lax.ppermute(up[0], "sec", RING_UP), lax.ppermute(down[1], "sec", RING_DOWN))

    left_all = lax.all_gather(left_table, "sec", axis_index_groups=GROUP_XC)
    send, meta, route, rlim, clim = pack(place, block_left, block_right, left_dims, right_dims, wavefunction)
    psi_slots = exchange_groups(send.reshape(NG, NZ, 2, WIDTH, WIDTH))
    meta_all = exchange_groups(meta.reshape(NG, NZ * 2)).reshape(-1)

    returned = []
    for deltas in CHUNKS:
        partial = contract(deltas, psi_slots, left_all, [rights[d] for d in deltas], meta_all)
        summed = lax.psum_scatter(
            partial.reshape(-1, WIDTH, WIDTH), "op", scatter_dimension=1, tiled=True
        )
        returned.append(exchange_groups(summed.reshape(NG, len(deltas), 2, ROWS, WIDTH)))

    sigma16, sigma32, sums = finish(place, route, rlim, clim, wavefunction, vectors, returned)
    values = jnp.sum(sums, axis=(1, 2))
    values = lax.psum(values, "sec", axis_index_groups=GROUP_XC)
    values = lax.psum(values, "op")
    values = lax.psum(values, "sec", axis_index_groups=GROUP_Z)
    theta = values[0] / values[1]
    residual = make_residual(
        place, rlim, clim, wavefunction, sigma32, jnp.full((1, WIDTH), 1.0, jnp.float32) * theta
    )
    return (sigma16, residual, values[2:])


def solution(mesh):
    placed = (
        P("sec", None, None),
        P(None, "sec", None, None),
        P("op", "sec", None, None),
        P("op", "sec", None, None),
        P("op", "sec"),
        P("op", "sec"),
        P("sec"),
        P(),
        P("sec"),
        P(),
    )
    return jax.shard_map(
        body,
        mesh=mesh,
        in_specs=placed,
        out_specs=(P("sec", "op", None), P("sec", "op", None), P()),
        check_vma=False,
    )
```

```python
import jax
import jax.numpy as jnp
from jax import lax
from jax.experimental import pallas as pl
from jax.experimental.pallas import tpu as pltpu
from jax.sharding import PartitionSpec as P

NX, NZ, NC, NY = 4, 8, 2, 4
NG = NX * NC
DEVICES = NX * NZ * NC * NY
BLOCKS, WIDTH, TERMS, SECTORS = 64, 128, 4, 16
ROWS = WIDTH // NY
PIECE = 4 * WIDTH
HEAD = 16
BATCH = 4
DEPTH = 3 * BATCH
CODE_BITS = 13.0
VMEM = 48 * 1024 * 1024
NOTHING = pl.CostEstimate(flops=1024, bytes_accessed=1024, transcendentals=0)


def sec_index(x, z, c):
    return (x * NZ + z) * NC + c


GROUP_XC = [[sec_index(x, z, c) for x in range(NX) for c in range(NC)] for z in range(NZ)]
GROUP_XCY = [
    [sec_index(x, z, c) * NY + y for x in range(NX) for c in range(NC) for y in range(NY)]
    for z in range(NZ)
]
RING_UP = [
    (sec_index(x, z, c), sec_index(x, (z + 1) % NZ, c))
    for x in range(NX)
    for z in range(NZ)
    for c in range(NC)
]
RING_DOWN = [(d, s) for s, d in RING_UP]
OP_UP = [(y, (y + 1) % NY) for y in range(NY)]
OP_DOWN = [(d, s) for s, d in OP_UP]
NEAR, MIDDLE, FAR = (0, 1, 7, 2, 6), (3, 5), (4,)


def smem():
    return pl.BlockSpec(memory_space=pltpu.SMEM)


def vmem():
    return pl.BlockSpec(memory_space=pltpu.VMEM)


def anywhere():
    return pl.BlockSpec(memory_space=pl.ANY)


def pack_kernel(
    place, block_left, block_right, left_dims, right_dims, psi, send, route, rlim, clim, count, codes
):
    sec = place[0]
    z_here = place[1]
    op = place[2]

    def clear(i, carry):
        count[i] = 0
        return carry

    lax.fori_loop(0, NX * NZ * NC, clear, 0)
    codes[...] = jnp.zeros_like(codes)
    rows = lax.broadcasted_iota(jnp.int32, (WIDTH, WIDTH), 0)
    cols = lax.broadcasted_iota(jnp.int32, (WIDTH, WIDTH), 1)

    def one(b, carry):
        left = block_left[b] - sec * SECTORS
        right = block_right[sec * BLOCKS + b]
        owner = lax.shift_right_logical(right, 4)
        rank = count[owner]
        count[owner] = rank + 1
        x_r = lax.shift_right_logical(owner, 4)
        z_r = lax.shift_right_logical(owner, 1) & 7
        group = x_r * 2 + (owner & 1)
        delta = (z_r - z_here) & 7
        route[b] = group * 16 + delta * 2 + rank
        rl = left_dims[left]
        cl = right_dims[right]
        rlim[b] = rl
        clim[b] = cl

        @pl.when(lax.shift_right_logical(delta, 1) == op)
        def _():
            sub = (delta & 1) * 2 + rank
            block = psi[b].astype(jnp.float32)
            live = (rows < rl) & (cols < cl)
            start = pl.multiple_of(sub * WIDTH, WIDTH)
            send[group, pl.ds(start, WIDTH)] = jnp.where(live, block, 0.0).astype(jnp.bfloat16)
            code = (left * 16 + (right & 15) + 1).astype(jnp.float32)
            codes[group, pl.ds(sub, 1)] = jnp.full((1, WIDTH), 1.0, jnp.float32) * code

        return carry

    lax.fori_loop(0, BLOCKS, one, 0)
    send[:, PIECE:] = codes[...].astype(jnp.bfloat16)


def pack(place, block_left, block_right, left_dims, right_dims, psi):
    return pl.pallas_call(
        pack_kernel,
        in_specs=[smem(), smem(), smem(), smem(), smem(), vmem()],
        out_specs=[vmem(), smem(), smem(), smem()],
        out_shape=[
            jax.ShapeDtypeStruct((NG, PIECE + HEAD, WIDTH), jnp.bfloat16),
            jax.ShapeDtypeStruct((BLOCKS,), jnp.int32),
            jax.ShapeDtypeStruct((BLOCKS,), jnp.int32),
            jax.ShapeDtypeStruct((BLOCKS,), jnp.int32),
        ],
        scratch_shapes=[
            pltpu.SMEM((NX * NZ * NC,), jnp.int32),
            pltpu.VMEM((NG, HEAD, WIDTH), jnp.float32),
        ],
        compiler_params=pltpu.CompilerParams(vmem_limit_bytes=VMEM),
        cost_estimate=NOTHING,
        name="pack",
    )(place, block_left, block_right, left_dims, right_dims, psi)


def contract(deltas, place, meta, pieces, left_all, rights, carried=None):
    slots = len(deltas) * 2
    most = NG * slots
    rows_own = slots * ROWS + HEAD
    rows_out = rows_own + (0 if carried is None else carried.shape[2])
    split = [len(r) for r in rights]

    def kernel(place, meta, own, below, above, far_low, far_high, left, *rest):
        right_refs, rest = rest[: sum(split)], rest[sum(split) :]
        if carried is not None:
            earlier, rest = rest[0], rest[1:]
        out, listed, psi_buf, left_buf, right_buf, heads, sems = rest
        op = place[2]
        heads[...] = jnp.zeros_like(heads)

        count = jnp.int32(0)
        for k, d in enumerate(deltas):
            relative = (d // 2 - op) & 3

            def scan(i, count):
                g = lax.shift_right_logical(i, 1)
                r = i & 1
                sub = (d & 1) * 2 + r
                code = meta[relative * NG * 4 + g * 4 + sub]

                @pl.when(code > 0)
                def _():
                    listed[count] = (
                        (code - 1) + g * 256 + (k * 2 + r) * 2048 + sub * 65536 + relative * 262144
                    )

                return count + (code > 0).astype(jnp.int32)

            count = lax.fori_loop(0, NG * 2, scan, count)

        def fields(entry):
            return (
                lax.shift_right_logical(entry, 4) & 15,
                entry & 15,
                lax.shift_right_logical(entry, 8) & 7,
                lax.shift_right_logical(entry, 11) & 15,
                lax.shift_right_logical(entry, 16) & 3,
                lax.shift_right_logical(entry, 18) & 3,
            )

        def psi_copy(ref, g, sub, at):
            start = pl.multiple_of(sub * WIDTH, WIDTH)
            return pltpu.make_async_copy(ref.at[g, pl.ds(start, WIDTH)], psi_buf.at[at], sems.at[at, 0])

        def left_copy(g, i, at):
            return pltpu.make_async_copy(left.at[g, :, i], left_buf.at[at], sems.at[at, 1])

        def fetch(n):
            i, j, g, s, sub, relative = fields(listed[n])
            at = lax.rem(n, DEPTH)
            left_copy(g, i, at).start()

            @pl.when(relative == 0)
            def _():
                psi_copy(own, g, sub, at).start()

            @pl.when(relative == 1)
            def _():
                psi_copy(above, g, sub, at).start()

            @pl.when(relative == 3)
            def _():
                psi_copy(below, g, sub, at).start()

            @pl.when((relative == 2) & (g < 4))
            def _():
                psi_copy(far_low, g, sub, at).start()

            @pl.when((relative == 2) & (g >= 4))
            def _():
                psi_copy(far_high, g - 4, sub, at).start()

            k = lax.shift_right_logical(s, 1)
            first = 0
            for n_delta, parts in enumerate(split):
                refs = right_refs[first : first + parts]
                first += parts

                @pl.when(k == n_delta)
                def _():
                    share = TERMS // parts
                    for p, ref in enumerate(refs):
                        pltpu.make_async_copy(
                            ref.at[:, j], right_buf.at[at, pl.ds(p * share, share)], sems.at[at, 2 + p]
                        ).start()

        def arrive(at):
            psi_copy(own, 0, 0, at).wait()
            left_copy(0, 0, at).wait()
            share = TERMS // split[0]
            for p in range(split[0]):
                pltpu.make_async_copy(
                    right_refs[p].at[:, 0], right_buf.at[at, pl.ds(p * share, share)], sems.at[at, 2 + p]
                ).wait()

        def begin(n, carry):
            fetch(n)
            return carry

        lax.fori_loop(0, jnp.minimum(count, 2 * BATCH), begin, 0)
        if carried is not None:
            for g in range(NG):
                out[g, :, rows_own:] = earlier[g]

        def step(m, carry):
            for q in range(BATCH):
                n = (m + 2) * BATCH + q

                @pl.when(n < count)
                def _():
                    fetch(n)

            for q in range(BATCH):
                n = m * BATCH + q

                @pl.when(n < count)
                def _():
                    arrive(lax.rem(n, DEPTH))

            results = []
            for q in range(BATCH):
                n = jnp.minimum(m * BATCH + q, count - 1)
                at = lax.rem(n, DEPTH)
                i, j, g, s, sub, relative = fields(listed[n])
                terms = lax.dot_general(
                    left_buf[at].reshape(TERMS * WIDTH, WIDTH),
                    psi_buf[at],
                    (((1,), (0,)), ((), ())),
                    preferred_element_type=jnp.float32,
                ).astype(jnp.bfloat16)
                total = None
                for a in range(0, TERMS, 2):
                    lhs = jnp.concatenate(
                        [terms[a * WIDTH : (a + 1) * WIDTH], terms[(a + 1) * WIDTH : (a + 2) * WIDTH]], axis=1
                    )
                    rhs = jnp.concatenate([right_buf[at, a], right_buf[at, a + 1]], axis=1)
                    part = lax.dot_general(
                        lhs, rhs, (((1,), (1,)), ((), ())), preferred_element_type=jnp.float32
                    )
                    total = part if total is None else total + part
                peak = jnp.max(jnp.max(jnp.abs(total), axis=0, keepdims=True), axis=1, keepdims=True)
                exponent = jnp.clip(jnp.floor(jnp.log2(peak)), -100.0, 127.0)
                code = jnp.round(total * jnp.exp2(CODE_BITS - exponent)).astype(jnp.int32).astype(jnp.int16)
                results.append((g, s, code, exponent))
            for g, s, code, exponent in results:
                start = pl.multiple_of(s * ROWS, ROWS)
                for y in range(NY):
                    out[g, y, pl.ds(start, ROWS)] = code[y * ROWS : (y + 1) * ROWS]
                heads[g, pl.ds(s, 1)] = jnp.broadcast_to(exponent, (1, WIDTH)).astype(jnp.int32)
            return carry

        lax.fori_loop(0, (count + BATCH - 1) // BATCH, step, 0)
        for y in range(NY):
            out[:, y, slots * ROWS : rows_own] = heads[...].astype(jnp.int16)

    flat = [part for r in rights for part in r]
    return pl.pallas_call(
        kernel,
        in_specs=[smem(), smem()]
        + [anywhere()] * (len(pieces) + 1 + len(flat))
        + ([] if carried is None else [vmem()]),
        out_specs=vmem(),
        out_shape=jax.ShapeDtypeStruct((NG, NY, rows_out, WIDTH), jnp.int16),
        scratch_shapes=[
            pltpu.SMEM((most,), jnp.int32),
            pltpu.VMEM((DEPTH, WIDTH, WIDTH), jnp.bfloat16),
            pltpu.VMEM((DEPTH, TERMS, WIDTH, WIDTH), jnp.bfloat16),
            pltpu.VMEM((DEPTH, TERMS, WIDTH, WIDTH), jnp.bfloat16),
            pltpu.VMEM((NG, HEAD, WIDTH), jnp.int32),
            pltpu.SemaphoreType.DMA((DEPTH, 4)),
        ],
        compiler_params=pltpu.CompilerParams(vmem_limit_bytes=VMEM),
        cost_estimate=pl.CostEstimate(
            flops=most * 16 * TERMS * 2 * WIDTH**3, bytes_accessed=most * 2**20, transcendentals=0
        ),
        name="contract",
    )(place, meta, *pieces, left_all, *flat, *([] if carried is None else [carried]))


def first_rows(chunks):
    origins = [0]
    for deltas in chunks:
        origins.append(origins[-1] + len(deltas) * 2 * ROWS + HEAD)
    return origins


def decode_kernel(chunks, last, place, route, rlim, clim, psi, vectors, *rest):
    returned, rest = rest[0], rest[1:]
    before, rest = (rest[0], rest[1:]) if last else (None, rest)
    (sigma32, result), scales = rest[:2], rest[2:]
    first_row = place[2] * ROWS
    rows = lax.broadcasted_iota(jnp.int32, (ROWS, WIDTH), 0) + first_row
    cols = lax.broadcasted_iota(jnp.int32, (ROWS, WIDTH), 1)
    origins = first_rows(chunks)
    for n, deltas in enumerate(chunks):
        top = origins[n] + len(deltas) * 2 * ROWS
        head = returned[:, top : top + HEAD].astype(jnp.int32).astype(jnp.float32)
        scales[n][...] = jnp.exp2(head - CODE_BITS)
    if last:
        result[...] = before[...]
    else:
        result[...] = jnp.zeros_like(result)

    def one(b, carry):
        slot = route[b]
        group = lax.shift_right_logical(slot, 4)
        delta = lax.shift_right_logical(slot, 1) & 7
        rank = slot & 1
        live = (rows < rlim[b]) & (cols < clim[b])
        amp = jnp.where(live, psi[b].astype(jnp.float32), 0.0)
        if not last:
            result[1] += amp * amp
        for n, deltas in enumerate(chunks):
            here = delta == deltas[0]
            place_in = jnp.int32(0)
            for k, d in enumerate(deltas[1:]):
                here = here | (delta == d)
                place_in = jnp.where(delta == d, k + 1, place_in)

            @pl.when(here)
            def _():
                s = place_in * 2 + rank
                start = pl.multiple_of(origins[n] + s * ROWS, HEAD)
                total = None
                for y in range(NY):
                    code = returned[group * NY + y, pl.ds(start, ROWS)]
                    part = code.astype(jnp.int32).astype(jnp.float32) * scales[n][group * NY + y, pl.ds(s, 1)]
                    total = part if total is None else total + part
                value = jnp.where(live, total, 0.0)
                sigma32[b] = value
                result[0] += amp * value
                result[2] += vectors[0, b].astype(jnp.float32) * value
                result[3] += vectors[1, b].astype(jnp.float32) * value

        return carry

    lax.fori_loop(0, BLOCKS, one, 0)


def spread_kernel(sums, spread):
    lane = lax.broadcasted_iota(jnp.int32, (1, WIDTH), 1)
    line = jnp.zeros((1, WIDTH), jnp.float32)
    for n in range(4):
        column = jnp.sum(sums[n], axis=0, keepdims=True)
        line = jnp.where(lane == n, jnp.sum(column, axis=1, keepdims=True), line)
    spread[...] = jnp.broadcast_to(line, (DEVICES, WIDTH))


def decode(chunks, place, route, rlim, clim, psi, vectors, returned, before=None):
    def whole(shape):
        return pl.BlockSpec(shape, lambda i, *_: (0,) * len(shape))

    part = (BLOCKS, ROWS, WIDTH)
    last = before is not None
    sums = (4, ROWS, WIDTH)

    def kernel(*refs):
        if not last:
            decode_kernel(chunks, last, *refs)
            return
        tail = len(chunks) + 1
        decode_kernel(chunks, last, *refs[: -tail - 1], refs[-1], *refs[-tail:-1])
        spread_kernel(refs[-1], refs[-tail - 1])

    return pl.pallas_call(
        kernel,
        grid_spec=pltpu.PrefetchScalarGridSpec(
            num_scalar_prefetch=4,
            grid=(1,),
            in_specs=[
                pl.BlockSpec(part, lambda i, place, *_: (0, place[2], 0)),
                pl.BlockSpec((2,) + part, lambda i, place, *_: (0, 0, place[2], 0)),
            ]
            + [whole(returned.shape)]
            + ([whole(sums)] if last else []),
            out_specs=[whole(part), whole((DEVICES, WIDTH)) if last else whole(sums)],
            scratch_shapes=[pltpu.VMEM((NG * NY, HEAD, WIDTH), jnp.float32) for _ in chunks]
            + ([pltpu.VMEM(sums, jnp.float32)] if last else []),
        ),
        out_shape=[
            jax.ShapeDtypeStruct(part, jnp.float32),
            jax.ShapeDtypeStruct((DEVICES, WIDTH) if last else sums, jnp.float32),
        ],
        compiler_params=pltpu.CompilerParams(vmem_limit_bytes=VMEM),
        cost_estimate=NOTHING,
        name="decode_last" if last else "decode",
    )(place, route, rlim, clim, psi, vectors, returned, *([before] if last else []))


def residual_kernel(place, route, rlim, clim, psi, near, distant, gathered, sigma16, out, products):
    first_row = place[2] * ROWS
    rows = lax.broadcasted_iota(jnp.int32, (ROWS, WIDTH), 0) + first_row
    cols = lax.broadcasted_iota(jnp.int32, (ROWS, WIDTH), 1)
    line = jnp.sum(gathered[...], axis=0, keepdims=True)
    lane = lax.broadcasted_iota(jnp.int32, (1, WIDTH), 1)
    cross = jnp.sum(jnp.where(lane == 0, line, 0.0), axis=1, keepdims=True)
    square = jnp.sum(jnp.where(lane == 1, line, 0.0), axis=1, keepdims=True)
    theta = jnp.broadcast_to(cross / square, (1, WIDTH))
    products[...] = line

    def one(b, carry):
        delta = lax.shift_right_logical(route[b], 1) & 7
        early = delta == NEAR[0]
        for d in NEAR[1:]:
            early = early | (delta == d)
        live = (rows < rlim[b]) & (cols < clim[b])
        amp = jnp.where(live, psi[b].astype(jnp.float32), 0.0)

        def emit(value):
            sigma16[b] = value.astype(jnp.bfloat16)
            out[b] = (value - theta * amp).astype(jnp.bfloat16)

        @pl.when(early)
        def _():
            emit(near[b])

        @pl.when(jnp.logical_not(early))
        def _():
            emit(distant[b])

        return carry

    lax.fori_loop(0, BLOCKS, one, 0)


def make_residual(place, route, rlim, clim, psi, near, distant, gathered):
    part = (BLOCKS, ROWS, WIDTH)

    def whole(shape):
        return pl.BlockSpec(shape, lambda i, *_: (0,) * len(shape))

    return pl.pallas_call(
        residual_kernel,
        grid_spec=pltpu.PrefetchScalarGridSpec(
            num_scalar_prefetch=4,
            grid=(1,),
            in_specs=[
                pl.BlockSpec(part, lambda i, place, *_: (0, place[2], 0)),
                whole(part),
                whole(part),
                whole((DEVICES, WIDTH)),
            ],
            out_specs=[whole(part), whole(part), whole((1, WIDTH))],
        ),
        out_shape=[
            jax.ShapeDtypeStruct(part, jnp.bfloat16),
            jax.ShapeDtypeStruct(part, jnp.bfloat16),
            jax.ShapeDtypeStruct((1, WIDTH), jnp.float32),
        ],
        compiler_params=pltpu.CompilerParams(vmem_limit_bytes=VMEM),
        cost_estimate=NOTHING,
        name="residual",
    )(place, route, rlim, clim, psi, near, distant, gathered)


def after(x, *others):
    return lax.optimization_barrier((x,) + others)[0]


def body(
    wavefunction,
    vectors,
    left_env,
    right_env,
    left_pattern,
    right_pattern,
    block_left,
    block_right,
    left_dims,
    right_dims,
):
    sec = lax.axis_index("sec").astype(jnp.int32)
    op = lax.axis_index("op").astype(jnp.int32)
    place = jnp.stack([sec, (sec // NC) % NZ, op]).astype(jnp.int32)

    right_table = right_env * right_pattern[:, :, None, None].astype(jnp.bfloat16)
    left_env = after(left_env, right_table)
    left_table = left_env * left_pattern[:, :, None, None].astype(jnp.bfloat16)
    rights = {0: (right_table,)}

    def ring(up, down):
        return lax.ppermute(up, "sec", RING_UP), lax.ppermute(down, "sec", RING_DOWN)

    up, down = ring(right_table, right_table)
    left_all = lax.all_gather(left_table, "sec", axis_index_groups=GROUP_XC)
    send, route, rlim, clim = pack(place, block_left, block_right, left_dims, right_dims, wavefunction)
    own = lax.all_to_all(send, "sec", 0, 0, axis_index_groups=GROUP_XC)
    below = lax.ppermute(own, "op", OP_UP)
    above = lax.ppermute(own, "op", OP_DOWN)
    up, down = after(up, own), after(down, own)
    rights[7], rights[1] = (up,), (down,)

    up, down = ring(up, down)
    far_low = lax.ppermute(below[:4], "op", OP_UP)
    far_high = lax.ppermute(above[4:], "op", OP_DOWN)
    up, down = after(up, far_low, far_high), after(down, far_low, far_high)
    rights[6], rights[2] = (up,), (down,)
    pieces = (own, below, above, far_low, far_high)
    heads = [p[:, PIECE : PIECE + 4, 0] for p in (own, above, jnp.concatenate([far_low, far_high]), below)]
    meta = jnp.stack(heads).astype(jnp.int32).reshape(-1)

    up, down = ring(up, down)

    def give_back(coded):
        coded = coded.reshape((NG * NY,) + coded.shape[2:])
        return lax.all_to_all(coded, ("sec", "op"), 0, 0, axis_index_groups=GROUP_XCY)

    near_codes = contract(NEAR, place, meta, pieces, left_all, [rights[d] for d in NEAR])
    rights[5], rights[3] = (up,), (down,)
    up, down = after(up, near_codes), after(down, near_codes)
    rights[4] = ring(up[:2], down[2:])
    near, sums = decode(
        (NEAR,), place, route, rlim, clim, wavefunction, vectors, give_back(near_codes)
    )
    middle_codes = contract(MIDDLE, place, meta, pieces, left_all, [rights[d] for d in MIDDLE])
    codes = contract(
        FAR, place, after(meta, sums), pieces, left_all, [rights[d] for d in FAR], middle_codes
    )
    distant, spread = decode(
        (FAR, MIDDLE), place, route, rlim, clim, wavefunction, vectors, give_back(codes), sums
    )
    gathered = lax.all_to_all(spread, ("sec", "op"), 0, 0, tiled=True)
    sigma16, residual, products = make_residual(
        place, route, rlim, clim, wavefunction, near, distant, gathered
    )
    return (sigma16, residual, products[0, 2:4])


def solution(mesh):
    placed = (
        P("sec", None, None),
        P(None, "sec", None, None),
        P("op", "sec", None, None),
        P("op", "sec", None, None),
        P("op", "sec"),
        P("op", "sec"),
        P("sec"),
        P(),
        P("sec"),
        P(),
    )
    return jax.shard_map(
        body,
        mesh=mesh,
        in_specs=placed,
        out_specs=(P("sec", "op", None), P("sec", "op", None), P()),
        check_vma=False,
    )
```

```python
import jax
import jax.numpy as jnp
from jax import lax
from jax.experimental import pallas as pl
from jax.experimental.pallas import tpu as pltpu
from jax.sharding import PartitionSpec as P

NX, NZ, NC, NY = 4, 8, 2, 4
NG = NX * NC
DEVICES = NX * NZ * NC * NY
BLOCKS, WIDTH, TERMS, SECTORS = 64, 128, 4, 16
ROWS = WIDTH // NY
PIECE = 4 * WIDTH
HEAD = 16
BATCH = 4
DEPTH = 3 * BATCH
CODE_BITS = 13.0
VMEM = 48 * 1024 * 1024
VMEM_ALL = 61 * 1024 * 1024
NOTHING = pl.CostEstimate(flops=1024, bytes_accessed=1024, transcendentals=0)


def sec_index(x, z, c):
    return (x * NZ + z) * NC + c


GROUP_XC = [[sec_index(x, z, c) for x in range(NX) for c in range(NC)] for z in range(NZ)]
GROUP_XCY = [
    [sec_index(x, z, c) * NY + y for x in range(NX) for c in range(NC) for y in range(NY)]
    for z in range(NZ)
]
RING_UP = [
    (sec_index(x, z, c), sec_index(x, (z + 1) % NZ, c))
    for x in range(NX)
    for z in range(NZ)
    for c in range(NC)
]
RING_DOWN = [(d, s) for s, d in RING_UP]
OP_UP = [(y, (y + 1) % NY) for y in range(NY)]
OP_DOWN = [(d, s) for s, d in OP_UP]
NEAR, MIDDLE, FAR = (0, 1, 7, 2, 6), (3, 5), (4,)


def smem():
    return pl.BlockSpec(memory_space=pltpu.SMEM)


def vmem():
    return pl.BlockSpec(memory_space=pltpu.VMEM)


def anywhere():
    return pl.BlockSpec(memory_space=pl.ANY)


def pack_kernel(
    place, block_left, block_right, left_dims, right_dims, psi, send, route, rlim, clim, count, codes
):
    sec = place[0]
    z_here = place[1]
    op = place[2]

    def clear(i, carry):
        count[i] = 0
        return carry

    lax.fori_loop(0, NX * NZ * NC, clear, 0)
    codes[...] = jnp.zeros_like(codes)
    rows = lax.broadcasted_iota(jnp.int32, (WIDTH, WIDTH), 0)
    cols = lax.broadcasted_iota(jnp.int32, (WIDTH, WIDTH), 1)

    def one(b, carry):
        left = block_left[b] - sec * SECTORS
        right = block_right[sec * BLOCKS + b]
        owner = lax.shift_right_logical(right, 4)
        rank = count[owner]
        count[owner] = rank + 1
        x_r = lax.shift_right_logical(owner, 4)
        z_r = lax.shift_right_logical(owner, 1) & 7
        group = x_r * 2 + (owner & 1)
        delta = (z_r - z_here) & 7
        route[b] = group * 16 + delta * 2 + rank
        rl = left_dims[left]
        cl = right_dims[right]
        rlim[b] = rl
        clim[b] = cl

        @pl.when(lax.shift_right_logical(delta, 1) == op)
        def _():
            sub = (delta & 1) * 2 + rank
            block = psi[b].astype(jnp.float32)
            live = (rows < rl) & (cols < cl)
            start = pl.multiple_of(sub * WIDTH, WIDTH)
            send[group, pl.ds(start, WIDTH)] = jnp.where(live, block, 0.0).astype(jnp.bfloat16)
            code = (left * 16 + (right & 15) + 1).astype(jnp.float32)
            codes[group, pl.ds(sub, 1)] = jnp.full((1, WIDTH), 1.0, jnp.float32) * code

        return carry

    lax.fori_loop(0, BLOCKS, one, 0)
    send[:, PIECE:] = codes[...].astype(jnp.bfloat16)


def pack(place, block_left, block_right, left_dims, right_dims, psi):
    return pl.pallas_call(
        pack_kernel,
        in_specs=[smem(), smem(), smem(), smem(), smem(), vmem()],
        out_specs=[vmem(), smem(), smem(), smem()],
        out_shape=[
            jax.ShapeDtypeStruct((NG, PIECE + HEAD, WIDTH), jnp.bfloat16),
            jax.ShapeDtypeStruct((BLOCKS,), jnp.int32),
            jax.ShapeDtypeStruct((BLOCKS,), jnp.int32),
            jax.ShapeDtypeStruct((BLOCKS,), jnp.int32),
        ],
        scratch_shapes=[
            pltpu.SMEM((NX * NZ * NC,), jnp.int32),
            pltpu.VMEM((NG, HEAD, WIDTH), jnp.float32),
        ],
        compiler_params=pltpu.CompilerParams(vmem_limit_bytes=VMEM),
        cost_estimate=NOTHING,
        name="pack",
    )(place, block_left, block_right, left_dims, right_dims, psi)


def contract(deltas, place, meta, pieces, left_all, rights, carried=None):
    slots = len(deltas) * 2
    most = NG * slots
    rows_own = slots * ROWS + HEAD
    rows_out = rows_own + (0 if carried is None else carried.shape[2])
    split = [len(r) for r in rights]

    def kernel(place, meta, own, below, above, far_low, far_high, left, *rest):
        right_refs, rest = rest[: sum(split)], rest[sum(split) :]
        if carried is not None:
            earlier, rest = rest[0], rest[1:]
        out, listed, psi_buf, left_buf, right_buf, heads, sems = rest
        op = place[2]
        heads[...] = jnp.zeros_like(heads)

        count = jnp.int32(0)
        for k, d in enumerate(deltas):
            relative = (d // 2 - op) & 3

            def scan(i, count):
                g = lax.shift_right_logical(i, 1)
                r = i & 1
                sub = (d & 1) * 2 + r
                code = meta[relative * NG * 4 + g * 4 + sub]

                @pl.when(code > 0)
                def _():
                    listed[count] = (
                        (code - 1) + g * 256 + (k * 2 + r) * 2048 + sub * 65536 + relative * 262144
                    )

                return count + (code > 0).astype(jnp.int32)

            count = lax.fori_loop(0, NG * 2, scan, count)

        def fields(entry):
            return (
                lax.shift_right_logical(entry, 4) & 15,
                entry & 15,
                lax.shift_right_logical(entry, 8) & 7,
                lax.shift_right_logical(entry, 11) & 15,
                lax.shift_right_logical(entry, 16) & 3,
                lax.shift_right_logical(entry, 18) & 3,
            )

        def psi_copy(ref, g, sub, at):
            start = pl.multiple_of(sub * WIDTH, WIDTH)
            return pltpu.make_async_copy(ref.at[g, pl.ds(start, WIDTH)], psi_buf.at[at], sems.at[at, 0])

        def left_copy(g, i, at):
            return pltpu.make_async_copy(left.at[g, :, i], left_buf.at[at], sems.at[at, 1])

        def fetch(n):
            i, j, g, s, sub, relative = fields(listed[n])
            at = lax.rem(n, DEPTH)
            left_copy(g, i, at).start()

            @pl.when(relative == 0)
            def _():
                psi_copy(own, g, sub, at).start()

            @pl.when(relative == 1)
            def _():
                psi_copy(above, g, sub, at).start()

            @pl.when(relative == 3)
            def _():
                psi_copy(below, g, sub, at).start()

            @pl.when((relative == 2) & (g < 4))
            def _():
                psi_copy(far_low, g, sub, at).start()

            @pl.when((relative == 2) & (g >= 4))
            def _():
                psi_copy(far_high, g - 4, sub, at).start()

            k = lax.shift_right_logical(s, 1)
            first = 0
            for n_delta, parts in enumerate(split):
                refs = right_refs[first : first + parts]
                first += parts

                @pl.when(k == n_delta)
                def _():
                    share = TERMS // parts
                    for p, ref in enumerate(refs):
                        pltpu.make_async_copy(
                            ref.at[:, j], right_buf.at[at, pl.ds(p * share, share)], sems.at[at, 2 + p]
                        ).start()

        def arrive(at):
            psi_copy(own, 0, 0, at).wait()
            left_copy(0, 0, at).wait()
            share = TERMS // split[0]
            for p in range(split[0]):
                pltpu.make_async_copy(
                    right_refs[p].at[:, 0], right_buf.at[at, pl.ds(p * share, share)], sems.at[at, 2 + p]
                ).wait()

        def begin(n, carry):
            fetch(n)
            return carry

        lax.fori_loop(0, jnp.minimum(count, 2 * BATCH), begin, 0)
        if carried is not None:
            for g in range(NG):
                out[g, :, rows_own:] = earlier[g]

        def step(m, carry):
            for q in range(BATCH):
                n = (m + 2) * BATCH + q

                @pl.when(n < count)
                def _():
                    fetch(n)

            for q in range(BATCH):
                n = m * BATCH + q

                @pl.when(n < count)
                def _():
                    arrive(lax.rem(n, DEPTH))

            results = []
            for q in range(BATCH):
                n = jnp.minimum(m * BATCH + q, count - 1)
                at = lax.rem(n, DEPTH)
                i, j, g, s, sub, relative = fields(listed[n])
                terms = lax.dot_general(
                    left_buf[at].reshape(TERMS * WIDTH, WIDTH),
                    psi_buf[at],
                    (((1,), (0,)), ((), ())),
                    preferred_element_type=jnp.float32,
                ).astype(jnp.bfloat16)
                total = None
                for a in range(0, TERMS, 2):
                    lhs = jnp.concatenate(
                        [terms[a * WIDTH : (a + 1) * WIDTH], terms[(a + 1) * WIDTH : (a + 2) * WIDTH]], axis=1
                    )
                    rhs = jnp.concatenate([right_buf[at, a], right_buf[at, a + 1]], axis=1)
                    part = lax.dot_general(
                        lhs, rhs, (((1,), (1,)), ((), ())), preferred_element_type=jnp.float32
                    )
                    total = part if total is None else total + part
                peak = jnp.max(jnp.max(jnp.abs(total), axis=0, keepdims=True), axis=1, keepdims=True)
                exponent = jnp.clip(jnp.floor(jnp.log2(peak)), -100.0, 127.0)
                code = jnp.round(total * jnp.exp2(CODE_BITS - exponent)).astype(jnp.int32).astype(jnp.int16)
                results.append((g, s, code, exponent))
            for g, s, code, exponent in results:
                start = pl.multiple_of(s * ROWS, ROWS)
                for y in range(NY):
                    out[g, y, pl.ds(start, ROWS)] = code[y * ROWS : (y + 1) * ROWS]
                heads[g, pl.ds(s, 1)] = jnp.broadcast_to(exponent, (1, WIDTH)).astype(jnp.int32)
            return carry

        lax.fori_loop(0, (count + BATCH - 1) // BATCH, step, 0)
        for y in range(NY):
            out[:, y, slots * ROWS : rows_own] = heads[...].astype(jnp.int16)

    flat = [part for r in rights for part in r]
    return pl.pallas_call(
        kernel,
        in_specs=[smem(), smem()]
        + [anywhere()] * (len(pieces) + 1 + len(flat))
        + ([] if carried is None else [vmem()]),
        out_specs=vmem(),
        out_shape=jax.ShapeDtypeStruct((NG, NY, rows_out, WIDTH), jnp.int16),
        scratch_shapes=[
            pltpu.SMEM((most,), jnp.int32),
            pltpu.VMEM((DEPTH, WIDTH, WIDTH), jnp.bfloat16),
            pltpu.VMEM((DEPTH, TERMS, WIDTH, WIDTH), jnp.bfloat16),
            pltpu.VMEM((DEPTH, TERMS, WIDTH, WIDTH), jnp.bfloat16),
            pltpu.VMEM((NG, HEAD, WIDTH), jnp.int32),
            pltpu.SemaphoreType.DMA((DEPTH, 4)),
        ],
        compiler_params=pltpu.CompilerParams(vmem_limit_bytes=VMEM_ALL),
        cost_estimate=pl.CostEstimate(
            flops=most * 16 * TERMS * 2 * WIDTH**3, bytes_accessed=most * 2**20, transcendentals=0
        ),
        name="contract",
    )(place, meta, *pieces, left_all, *flat, *([] if carried is None else [carried]))


def first_rows(chunks):
    origins = [0]
    for deltas in chunks:
        origins.append(origins[-1] + len(deltas) * 2 * ROWS + HEAD)
    return origins


def decode_kernel(chunks, later, place, route, rlim, clim, psi, vectors, *rest):
    returned, rest = rest[0], rest[1:]
    before, rest = (rest[0], rest[1:]) if later else (None, rest)
    (sigma32, result), scales = rest[:2], rest[2:]
    first_row = place[2] * ROWS
    rows = lax.broadcasted_iota(jnp.int32, (ROWS, WIDTH), 0) + first_row
    cols = lax.broadcasted_iota(jnp.int32, (ROWS, WIDTH), 1)
    origins = first_rows(chunks)
    for n, deltas in enumerate(chunks):
        top = origins[n] + len(deltas) * 2 * ROWS
        head = returned[:, top : top + HEAD].astype(jnp.int32).astype(jnp.float32)
        scales[n][...] = jnp.exp2(head - CODE_BITS)
    if later:
        result[...] = before[...]
    else:
        result[...] = jnp.zeros_like(result)

    def one(b, carry):
        slot = route[b]
        group = lax.shift_right_logical(slot, 4)
        delta = lax.shift_right_logical(slot, 1) & 7
        rank = slot & 1
        live = (rows < rlim[b]) & (cols < clim[b])
        amp = jnp.where(live, psi[b].astype(jnp.float32), 0.0)
        if not later:
            result[1] += amp * amp
        for n, deltas in enumerate(chunks):
            here = delta == deltas[0]
            place_in = jnp.int32(0)
            for k, d in enumerate(deltas[1:]):
                here = here | (delta == d)
                place_in = jnp.where(delta == d, k + 1, place_in)

            @pl.when(here)
            def _():
                s = place_in * 2 + rank
                start = pl.multiple_of(origins[n] + s * ROWS, HEAD)
                total = None
                for y in range(NY):
                    code = returned[group * NY + y, pl.ds(start, ROWS)]
                    part = code.astype(jnp.int32).astype(jnp.float32) * scales[n][group * NY + y, pl.ds(s, 1)]
                    total = part if total is None else total + part
                value = jnp.where(live, total, 0.0)
                sigma32[b] = value
                result[0] += amp * value
                result[2] += vectors[0, b].astype(jnp.float32) * value
                result[3] += vectors[1, b].astype(jnp.float32) * value

        return carry

    lax.fori_loop(0, BLOCKS, one, 0)


def spread_kernel(sums, spread):
    lane = lax.broadcasted_iota(jnp.int32, (1, WIDTH), 1)
    line = jnp.zeros((1, WIDTH), jnp.float32)
    for n in range(4):
        column = jnp.sum(sums[n], axis=0, keepdims=True)
        line = jnp.where(lane == n, jnp.sum(column, axis=1, keepdims=True), line)
    spread[...] = jnp.broadcast_to(line[:, :8], (DEVICES, 8))


def decode(chunks, place, route, rlim, clim, psi, vectors, returned, before=None, last=False):
    def whole(shape):
        return pl.BlockSpec(shape, lambda i, *_: (0,) * len(shape))

    part = (BLOCKS, ROWS, WIDTH)
    later = before is not None
    sums = (4, ROWS, WIDTH)

    def kernel(*refs):
        if not last:
            decode_kernel(chunks, later, *refs)
            return
        tail = len(chunks) + 1
        decode_kernel(chunks, later, *refs[: -tail - 1], refs[-1], *refs[-tail:-1])
        spread_kernel(refs[-1], refs[-tail - 1])

    return pl.pallas_call(
        kernel,
        grid_spec=pltpu.PrefetchScalarGridSpec(
            num_scalar_prefetch=4,
            grid=(1,),
            in_specs=[
                pl.BlockSpec(part, lambda i, place, *_: (0, place[2], 0)),
                pl.BlockSpec((2,) + part, lambda i, place, *_: (0, 0, place[2], 0)),
            ]
            + [whole(returned.shape)]
            + ([whole(sums)] if later else []),
            out_specs=[whole(part), whole((DEVICES, 8)) if last else whole(sums)],
            scratch_shapes=[pltpu.VMEM((NG * NY, HEAD, WIDTH), jnp.float32) for _ in chunks]
            + ([pltpu.VMEM(sums, jnp.float32)] if last else []),
        ),
        out_shape=[
            jax.ShapeDtypeStruct(part, jnp.float32),
            jax.ShapeDtypeStruct((DEVICES, 8) if last else sums, jnp.float32),
        ],
        compiler_params=pltpu.CompilerParams(vmem_limit_bytes=VMEM),
        cost_estimate=NOTHING,
        name="decode_last" if last else "decode",
    )(place, route, rlim, clim, psi, vectors, returned, *([before] if later else []))


def residual_kernel(place, route, rlim, clim, psi, near, middle, far, gathered, sigma16, out, products):
    first_row = place[2] * ROWS
    rows = lax.broadcasted_iota(jnp.int32, (ROWS, WIDTH), 0) + first_row
    cols = lax.broadcasted_iota(jnp.int32, (ROWS, WIDTH), 1)
    line = jnp.sum(gathered[...], axis=0, keepdims=True)
    lane = lax.broadcasted_iota(jnp.int32, (1, 8), 1)
    cross = jnp.sum(jnp.where(lane == 0, line, 0.0), axis=1, keepdims=True)
    square = jnp.sum(jnp.where(lane == 1, line, 0.0), axis=1, keepdims=True)
    theta = jnp.broadcast_to(cross / square, (1, WIDTH))
    products[...] = line

    def one(b, carry):
        delta = lax.shift_right_logical(route[b], 1) & 7
        in_middle = (delta == MIDDLE[0]) | (delta == MIDDLE[1])
        in_far = delta == FAR[0]
        live = (rows < rlim[b]) & (cols < clim[b])
        amp = jnp.where(live, psi[b].astype(jnp.float32), 0.0)

        def emit(value):
            sigma16[b] = value.astype(jnp.bfloat16)
            out[b] = (value - theta * amp).astype(jnp.bfloat16)

        @pl.when(in_far)
        def _():
            emit(far[b])

        @pl.when(in_middle)
        def _():
            emit(middle[b])

        @pl.when(jnp.logical_not(in_far | in_middle))
        def _():
            emit(near[b])

        return carry

    lax.fori_loop(0, BLOCKS, one, 0)


def make_residual(place, route, rlim, clim, psi, near, middle, far, gathered):
    part = (BLOCKS, ROWS, WIDTH)

    def whole(shape):
        return pl.BlockSpec(shape, lambda i, *_: (0,) * len(shape))

    return pl.pallas_call(
        residual_kernel,
        grid_spec=pltpu.PrefetchScalarGridSpec(
            num_scalar_prefetch=4,
            grid=(1,),
            in_specs=[
                pl.BlockSpec(part, lambda i, place, *_: (0, place[2], 0)),
                whole(part),
                whole(part),
                whole(part),
                whole((DEVICES, 8)),
            ],
            out_specs=[whole(part), whole(part), whole((1, 8))],
        ),
        out_shape=[
            jax.ShapeDtypeStruct(part, jnp.bfloat16),
            jax.ShapeDtypeStruct(part, jnp.bfloat16),
            jax.ShapeDtypeStruct((1, 8), jnp.float32),
        ],
        compiler_params=pltpu.CompilerParams(vmem_limit_bytes=VMEM),
        cost_estimate=NOTHING,
        name="residual",
    )(place, route, rlim, clim, psi, near, middle, far, gathered)


def halve_kernel(up, down, low, high, buf, sems):
    half = TERMS // 2
    arrive, leave = [], []
    for t in range(half):
        for n, (source, first, target) in enumerate(((up, 0, low), (down, half, high))):
            at = 2 * t + n
            arrive.append(pltpu.make_async_copy(source.at[first + t], buf.at[at], sems.at[0, at]))
            leave.append(pltpu.make_async_copy(buf.at[at], target.at[t], sems.at[1, at]))
    for c in arrive:
        c.start()
    for c, d in zip(arrive, leave):
        c.wait()
        d.start()
    for d in leave:
        d.wait()


def halve(up, down):
    shape = jax.ShapeDtypeStruct((TERMS // 2,) + up.shape[1:], up.dtype)
    return pl.pallas_call(
        halve_kernel,
        in_specs=[anywhere(), anywhere()],
        out_specs=[anywhere(), anywhere()],
        out_shape=[shape, shape],
        scratch_shapes=[
            pltpu.VMEM((TERMS,) + up.shape[1:], up.dtype),
            pltpu.SemaphoreType.DMA((2, TERMS)),
        ],
        compiler_params=pltpu.CompilerParams(vmem_limit_bytes=VMEM),
        cost_estimate=NOTHING,
        name="halve",
    )(up, down)


def after(x, *others):
    return lax.optimization_barrier((x,) + others)[0]


def body(
    wavefunction,
    vectors,
    left_env,
    right_env,
    left_pattern,
    right_pattern,
    block_left,
    block_right,
    left_dims,
    right_dims,
):
    sec = lax.axis_index("sec").astype(jnp.int32)
    op = lax.axis_index("op").astype(jnp.int32)
    place = jnp.stack([sec, (sec // NC) % NZ, op]).astype(jnp.int32)

    right_table = right_env * right_pattern[:, :, None, None].astype(jnp.bfloat16)
    left_env = after(left_env, right_table)
    left_table = left_env * left_pattern[:, :, None, None].astype(jnp.bfloat16)
    rights = {0: (right_table,)}

    def ring(up, down):
        return lax.ppermute(up, "sec", RING_UP), lax.ppermute(down, "sec", RING_DOWN)

    up, down = ring(right_table, right_table)
    left_all = lax.all_gather(left_table, "sec", axis_index_groups=GROUP_XC)
    send, route, rlim, clim = pack(place, block_left, block_right, left_dims, right_dims, wavefunction)
    own = lax.all_to_all(send, "sec", 0, 0, axis_index_groups=GROUP_XC)
    below = lax.ppermute(own, "op", OP_UP)
    above = lax.ppermute(own, "op", OP_DOWN)
    up, down = after(up, own), after(down, own)
    rights[7], rights[1] = (up,), (down,)

    up, down = ring(up, down)
    far_low = lax.ppermute(below[:4], "op", OP_UP)
    far_high = lax.ppermute(above[4:], "op", OP_DOWN)
    up, down = after(up, far_low, far_high), after(down, far_low, far_high)
    rights[6], rights[2] = (up,), (down,)
    pieces = (own, below, above, far_low, far_high)
    heads = [p[:, PIECE : PIECE + 4, 0] for p in (own, above, jnp.concatenate([far_low, far_high]), below)]
    meta = jnp.stack(heads).astype(jnp.int32).reshape(-1)

    up, down = ring(up, down)

    def give_back(coded):
        coded = coded.reshape((NG * NY,) + coded.shape[2:])
        return lax.all_to_all(coded, ("sec", "op"), 0, 0, axis_index_groups=GROUP_XCY)

    near_codes = contract(NEAR, place, meta, pieces, left_all, [rights[d] for d in NEAR])
    rights[5], rights[3] = (up,), (down,)
    up, down = after(up, near_codes), after(down, near_codes)
    rights[4] = ring(*halve(up, down))
    near_back = give_back(near_codes)
    near, sums = decode((NEAR,), place, route, rlim, clim, wavefunction, vectors, near_back)
    middle_codes = contract(MIDDLE, place, meta, pieces, left_all, [rights[d] for d in MIDDLE])
    middle_back = give_back(after(middle_codes, near_back))
    far_codes = contract(FAR, place, meta, pieces, left_all, [rights[d] for d in FAR])
    middle, sums = decode(
        (MIDDLE,), place, route, rlim, clim, wavefunction, vectors, middle_back, sums
    )
    far_back = give_back(after(far_codes, middle_back))
    far, spread = decode((FAR,), place, route, rlim, clim, wavefunction, vectors, far_back, sums, True)
    gathered = lax.all_to_all(spread, ("sec", "op"), 0, 0, tiled=True)
    sigma16, residual, products = make_residual(
        place, route, rlim, clim, wavefunction, near, middle, far, gathered
    )
    return (sigma16, residual, products[0, 2:4])


def solution(mesh):
    placed = (
        P("sec", None, None),
        P(None, "sec", None, None),
        P("op", "sec", None, None),
        P("op", "sec", None, None),
        P("op", "sec"),
        P("op", "sec"),
        P("sec"),
        P(),
        P("sec"),
        P(),
    )
    return jax.shard_map(
        body,
        mesh=mesh,
        in_specs=placed,
        out_specs=(P("sec", "op", None), P("sec", "op", None), P()),
        check_vma=False,
    )
```

```python
import jax
import jax.numpy as jnp
from jax import lax
from jax.experimental import pallas as pl
from jax.experimental.pallas import tpu as pltpu
from jax.sharding import PartitionSpec as P

NX, NZ, NC, NY = 4, 8, 2, 4
NG = NX * NC
DEVICES = NX * NZ * NC * NY
BLOCKS, WIDTH, TERMS, SECTORS = 64, 128, 4, 16
ROWS = WIDTH // NY
PIECE = 4 * WIDTH
HEAD = 16
BATCH = 8
DEPTH = 3 * BATCH
CODE_BITS = 13.0
VMEM = 48 * 1024 * 1024
VMEM_ALL = 61 * 1024 * 1024
NOTHING = pl.CostEstimate(flops=1024, bytes_accessed=1024, transcendentals=0)


def sec_index(x, z, c):
    return (x * NZ + z) * NC + c


GROUP_XC = [[sec_index(x, z, c) for x in range(NX) for c in range(NC)] for z in range(NZ)]
GROUP_XCY = [
    [sec_index(x, z, c) * NY + y for x in range(NX) for c in range(NC) for y in range(NY)]
    for z in range(NZ)
]
RING_UP = [
    (sec_index(x, z, c), sec_index(x, (z + 1) % NZ, c))
    for x in range(NX)
    for z in range(NZ)
    for c in range(NC)
]
RING_DOWN = [(d, s) for s, d in RING_UP]
OP_UP = [(y, (y + 1) % NY) for y in range(NY)]
OP_DOWN = [(d, s) for s, d in OP_UP]
NEAR, MIDDLE, FAR = (0, 1, 7, 2, 6), (3, 5), (4,)


def smem():
    return pl.BlockSpec(memory_space=pltpu.SMEM)


def vmem():
    return pl.BlockSpec(memory_space=pltpu.VMEM)


def anywhere():
    return pl.BlockSpec(memory_space=pl.ANY)


def pack_kernel(
    place, block_left, block_right, left_dims, right_dims, psi, send, route, rlim, clim, count, codes
):
    sec = place[0]
    z_here = place[1]
    op = place[2]

    def clear(i, carry):
        count[i] = 0
        return carry

    lax.fori_loop(0, NX * NZ * NC, clear, 0)
    codes[...] = jnp.zeros_like(codes)
    rows = lax.broadcasted_iota(jnp.int32, (WIDTH, WIDTH), 0)
    cols = lax.broadcasted_iota(jnp.int32, (WIDTH, WIDTH), 1)

    def one(b, carry):
        left = block_left[b] - sec * SECTORS
        right = block_right[sec * BLOCKS + b]
        owner = lax.shift_right_logical(right, 4)
        rank = count[owner]
        count[owner] = rank + 1
        x_r = lax.shift_right_logical(owner, 4)
        z_r = lax.shift_right_logical(owner, 1) & 7
        group = x_r * 2 + (owner & 1)
        delta = (z_r - z_here) & 7
        route[b] = group * 16 + delta * 2 + rank
        rl = left_dims[left]
        cl = right_dims[right]
        rlim[b] = rl
        clim[b] = cl

        @pl.when(lax.shift_right_logical(delta, 1) == op)
        def _():
            sub = (delta & 1) * 2 + rank
            block = psi[b].astype(jnp.float32)
            live = (rows < rl) & (cols < cl)
            start = pl.multiple_of(sub * WIDTH, WIDTH)
            send[group, pl.ds(start, WIDTH)] = jnp.where(live, block, 0.0).astype(jnp.bfloat16)
            code = (left * 16 + (right & 15) + 1).astype(jnp.float32)
            codes[group, pl.ds(sub, 1)] = jnp.full((1, WIDTH), 1.0, jnp.float32) * code

        return carry

    lax.fori_loop(0, BLOCKS, one, 0)
    send[:, PIECE:] = codes[...].astype(jnp.bfloat16)


def pack(place, block_left, block_right, left_dims, right_dims, psi):
    return pl.pallas_call(
        pack_kernel,
        in_specs=[smem(), smem(), smem(), smem(), smem(), vmem()],
        out_specs=[vmem(), smem(), smem(), smem()],
        out_shape=[
            jax.ShapeDtypeStruct((NG, PIECE + HEAD, WIDTH), jnp.bfloat16),
            jax.ShapeDtypeStruct((BLOCKS,), jnp.int32),
            jax.ShapeDtypeStruct((BLOCKS,), jnp.int32),
            jax.ShapeDtypeStruct((BLOCKS,), jnp.int32),
        ],
        scratch_shapes=[
            pltpu.SMEM((NX * NZ * NC,), jnp.int32),
            pltpu.VMEM((NG, HEAD, WIDTH), jnp.float32),
        ],
        compiler_params=pltpu.CompilerParams(vmem_limit_bytes=VMEM),
        cost_estimate=NOTHING,
        name="pack",
    )(place, block_left, block_right, left_dims, right_dims, psi)


def contract(deltas, place, meta, pieces, left_all, rights, carried=None):
    slots = len(deltas) * 2
    most = NG * slots
    rows_own = slots * ROWS + HEAD
    rows_out = rows_own + (0 if carried is None else carried.shape[2])
    split = [len(r) for r in rights]

    def kernel(place, meta, own, below, above, far_low, far_high, left, *rest):
        right_refs, rest = rest[: sum(split)], rest[sum(split) :]
        if carried is not None:
            earlier, rest = rest[0], rest[1:]
        out, listed, psi_buf, left_buf, right_buf, heads, sems = rest
        op = place[2]
        heads[...] = jnp.zeros_like(heads)

        count = jnp.int32(0)
        for k, d in enumerate(deltas):
            relative = (d // 2 - op) & 3

            def scan(i, count):
                g = lax.shift_right_logical(i, 1)
                r = i & 1
                sub = (d & 1) * 2 + r
                code = meta[relative * NG * 4 + g * 4 + sub]

                @pl.when(code > 0)
                def _():
                    listed[count] = (
                        (code - 1) + g * 256 + (k * 2 + r) * 2048 + sub * 65536 + relative * 262144
                    )

                return count + (code > 0).astype(jnp.int32)

            count = lax.fori_loop(0, NG * 2, scan, count)

        def fields(entry):
            return (
                lax.shift_right_logical(entry, 4) & 15,
                entry & 15,
                lax.shift_right_logical(entry, 8) & 7,
                lax.shift_right_logical(entry, 11) & 15,
                lax.shift_right_logical(entry, 16) & 3,
                lax.shift_right_logical(entry, 18) & 3,
            )

        def psi_copy(ref, g, sub, at):
            start = pl.multiple_of(sub * WIDTH, WIDTH)
            return pltpu.make_async_copy(ref.at[g, pl.ds(start, WIDTH)], psi_buf.at[at], sems.at[at, 0])

        def left_copy(g, i, at):
            return pltpu.make_async_copy(left.at[g, :, i], left_buf.at[at], sems.at[at, 1])

        def fetch(n):
            i, j, g, s, sub, relative = fields(listed[n])
            at = lax.rem(n, DEPTH)
            left_copy(g, i, at).start()

            @pl.when(relative == 0)
            def _():
                psi_copy(own, g, sub, at).start()

            @pl.when(relative == 1)
            def _():
                psi_copy(above, g, sub, at).start()

            @pl.when(relative == 3)
            def _():
                psi_copy(below, g, sub, at).start()

            @pl.when((relative == 2) & (g < 4))
            def _():
                psi_copy(far_low, g, sub, at).start()

            @pl.when((relative == 2) & (g >= 4))
            def _():
                psi_copy(far_high, g - 4, sub, at).start()

            k = lax.shift_right_logical(s, 1)
            first = 0
            for n_delta, parts in enumerate(split):
                refs = right_refs[first : first + parts]
                first += parts

                @pl.when(k == n_delta)
                def _():
                    share = TERMS // parts
                    for p, ref in enumerate(refs):
                        pltpu.make_async_copy(
                            ref.at[:, j], right_buf.at[at, pl.ds(p * share, share)], sems.at[at, 2 + p]
                        ).start()

        def arrive(at):
            psi_copy(own, 0, 0, at).wait()
            left_copy(0, 0, at).wait()
            share = TERMS // split[0]
            for p in range(split[0]):
                pltpu.make_async_copy(
                    right_refs[p].at[:, 0], right_buf.at[at, pl.ds(p * share, share)], sems.at[at, 2 + p]
                ).wait()

        def begin(n, carry):
            fetch(n)
            return carry

        lax.fori_loop(0, jnp.minimum(count, 2 * BATCH), begin, 0)
        if carried is not None:
            for g in range(NG):
                out[g, :, rows_own:] = earlier[g]

        def step(m, carry):
            for q in range(BATCH):
                n = (m + 2) * BATCH + q

                @pl.when(n < count)
                def _():
                    fetch(n)

            for q in range(BATCH):
                n = m * BATCH + q

                @pl.when(n < count)
                def _():
                    arrive(lax.rem(n, DEPTH))

            results = []
            for q in range(BATCH):
                n = jnp.minimum(m * BATCH + q, count - 1)
                at = lax.rem(n, DEPTH)
                i, j, g, s, sub, relative = fields(listed[n])
                terms = lax.dot_general(
                    left_buf[at].reshape(TERMS * WIDTH, WIDTH),
                    psi_buf[at],
                    (((1,), (0,)), ((), ())),
                    preferred_element_type=jnp.float32,
                ).astype(jnp.bfloat16)
                total = None
                for a in range(0, TERMS, 2):
                    lhs = jnp.concatenate(
                        [terms[a * WIDTH : (a + 1) * WIDTH], terms[(a + 1) * WIDTH : (a + 2) * WIDTH]], axis=1
                    )
                    rhs = jnp.concatenate([right_buf[at, a], right_buf[at, a + 1]], axis=1)
                    part = lax.dot_general(
                        lhs, rhs, (((1,), (1,)), ((), ())), preferred_element_type=jnp.float32
                    )
                    total = part if total is None else total + part
                peak = jnp.max(jnp.max(jnp.abs(total), axis=0, keepdims=True), axis=1, keepdims=True)
                exponent = jnp.clip(jnp.floor(jnp.log2(peak)), -100.0, 127.0)
                code = jnp.round(total * jnp.exp2(CODE_BITS - exponent)).astype(jnp.int32).astype(jnp.int16)
                results.append((g, s, code, exponent))
            for g, s, code, exponent in results:
                start = pl.multiple_of(s * ROWS, ROWS)
                for y in range(NY):
                    out[g, y, pl.ds(start, ROWS)] = code[y * ROWS : (y + 1) * ROWS]
                heads[g, pl.ds(s, 1)] = jnp.broadcast_to(exponent, (1, WIDTH)).astype(jnp.int32)
            return carry

        lax.fori_loop(0, (count + BATCH - 1) // BATCH, step, 0)
        for y in range(NY):
            out[:, y, slots * ROWS : rows_own] = heads[...].astype(jnp.int16)

    flat = [part for r in rights for part in r]
    return pl.pallas_call(
        kernel,
        in_specs=[smem(), smem()]
        + [anywhere()] * (len(pieces) + 1 + len(flat))
        + ([] if carried is None else [vmem()]),
        out_specs=vmem(),
        out_shape=jax.ShapeDtypeStruct((NG, NY, rows_out, WIDTH), jnp.int16),
        scratch_shapes=[
            pltpu.SMEM((most,), jnp.int32),
            pltpu.VMEM((DEPTH, WIDTH, WIDTH), jnp.bfloat16),
            pltpu.VMEM((DEPTH, TERMS, WIDTH, WIDTH), jnp.bfloat16),
            pltpu.VMEM((DEPTH, TERMS, WIDTH, WIDTH), jnp.bfloat16),
            pltpu.VMEM((NG, HEAD, WIDTH), jnp.int32),
            pltpu.SemaphoreType.DMA((DEPTH, 4)),
        ],
        compiler_params=pltpu.CompilerParams(vmem_limit_bytes=VMEM_ALL),
        cost_estimate=pl.CostEstimate(
            flops=most * 16 * TERMS * 2 * WIDTH**3, bytes_accessed=most * 2**20, transcendentals=0
        ),
        name="contract",
    )(place, meta, *pieces, left_all, *flat, *([] if carried is None else [carried]))


def first_rows(chunks):
    origins = [0]
    for deltas in chunks:
        origins.append(origins[-1] + len(deltas) * 2 * ROWS + HEAD)
    return origins


def decode_kernel(chunks, later, place, route, rlim, clim, psi, vectors, *rest):
    returned, rest = rest[0], rest[1:]
    before, rest = (rest[0], rest[1:]) if later else (None, rest)
    (sigma32, result), scales = rest[:2], rest[2:]
    first_row = place[2] * ROWS
    rows = lax.broadcasted_iota(jnp.int32, (ROWS, WIDTH), 0) + first_row
    cols = lax.broadcasted_iota(jnp.int32, (ROWS, WIDTH), 1)
    origins = first_rows(chunks)
    for n, deltas in enumerate(chunks):
        top = origins[n] + len(deltas) * 2 * ROWS
        head = returned[:, top : top + HEAD].astype(jnp.int32).astype(jnp.float32)
        scales[n][...] = jnp.exp2(head - CODE_BITS)
    if later:
        result[...] = before[...]
    else:
        result[...] = jnp.zeros_like(result)

    def one(b, carry):
        slot = route[b]
        group = lax.shift_right_logical(slot, 4)
        delta = lax.shift_right_logical(slot, 1) & 7
        rank = slot & 1
        live = (rows < rlim[b]) & (cols < clim[b])
        amp = jnp.where(live, psi[b].astype(jnp.float32), 0.0)
        if not later:
            result[1] += amp * amp
        for n, deltas in enumerate(chunks):
            here = delta == deltas[0]
            place_in = jnp.int32(0)
            for k, d in enumerate(deltas[1:]):
                here = here | (delta == d)
                place_in = jnp.where(delta == d, k + 1, place_in)

            @pl.when(here)
            def _():
                s = place_in * 2 + rank
                start = pl.multiple_of(origins[n] + s * ROWS, HEAD)
                total = None
                for y in range(NY):
                    code = returned[group * NY + y, pl.ds(start, ROWS)]
                    part = code.astype(jnp.int32).astype(jnp.float32) * scales[n][group * NY + y, pl.ds(s, 1)]
                    total = part if total is None else total + part
                value = jnp.where(live, total, 0.0)
                sigma32[b] = value
                result[0] += amp * value
                result[2] += vectors[0, b].astype(jnp.float32) * value
                result[3] += vectors[1, b].astype(jnp.float32) * value

        return carry

    lax.fori_loop(0, BLOCKS, one, 0)


def spread_kernel(sums, spread):
    lane = lax.broadcasted_iota(jnp.int32, (1, WIDTH), 1)
    line = jnp.zeros((1, WIDTH), jnp.float32)
    for n in range(4):
        column = jnp.sum(sums[n], axis=0, keepdims=True)
        line = jnp.where(lane == n, jnp.sum(column, axis=1, keepdims=True), line)
    spread[...] = jnp.broadcast_to(line[:, :8], (DEVICES, 8))


def decode(chunks, place, route, rlim, clim, psi, vectors, returned, before=None, last=False):
    def whole(shape):
        return pl.BlockSpec(shape, lambda i, *_: (0,) * len(shape))

    part = (BLOCKS, ROWS, WIDTH)
    later = before is not None
    sums = (4, ROWS, WIDTH)

    def kernel(*refs):
        if not last:
            decode_kernel(chunks, later, *refs)
            return
        tail = len(chunks) + 1
        decode_kernel(chunks, later, *refs[: -tail - 1], refs[-1], *refs[-tail:-1])
        spread_kernel(refs[-1], refs[-tail - 1])

    return pl.pallas_call(
        kernel,
        grid_spec=pltpu.PrefetchScalarGridSpec(
            num_scalar_prefetch=4,
            grid=(1,),
            in_specs=[
                pl.BlockSpec(part, lambda i, place, *_: (0, place[2], 0)),
                pl.BlockSpec((2,) + part, lambda i, place, *_: (0, 0, place[2], 0)),
            ]
            + [whole(returned.shape)]
            + ([whole(sums)] if later else []),
            out_specs=[whole(part), whole((DEVICES, 8)) if last else whole(sums)],
            scratch_shapes=[pltpu.VMEM((NG * NY, HEAD, WIDTH), jnp.float32) for _ in chunks]
            + ([pltpu.VMEM(sums, jnp.float32)] if last else []),
        ),
        out_shape=[
            jax.ShapeDtypeStruct(part, jnp.float32),
            jax.ShapeDtypeStruct((DEVICES, 8) if last else sums, jnp.float32),
        ],
        compiler_params=pltpu.CompilerParams(vmem_limit_bytes=VMEM),
        cost_estimate=NOTHING,
        name="decode_last" if last else "decode",
    )(place, route, rlim, clim, psi, vectors, returned, *([before] if later else []))


def prepare_kernel(place, route, rlim, clim, psi, near, middle, far, sigma16, sigma32, amplitude):
    first_row = place[2] * ROWS
    rows = lax.broadcasted_iota(jnp.int32, (ROWS, WIDTH), 0) + first_row
    cols = lax.broadcasted_iota(jnp.int32, (ROWS, WIDTH), 1)

    def one(b, carry):
        delta = lax.shift_right_logical(route[b], 1) & 7
        in_middle = (delta == MIDDLE[0]) | (delta == MIDDLE[1])
        in_far = delta == FAR[0]
        live = (rows < rlim[b]) & (cols < clim[b])
        amplitude[b] = jnp.where(live, psi[b].astype(jnp.float32), 0.0).astype(jnp.bfloat16)

        def emit(value):
            sigma32[b] = value
            sigma16[b] = value.astype(jnp.bfloat16)

        @pl.when(in_far)
        def _():
            emit(far[b])

        @pl.when(in_middle)
        def _():
            emit(middle[b])

        @pl.when(jnp.logical_not(in_far | in_middle))
        def _():
            emit(near[b])

        return carry

    lax.fori_loop(0, BLOCKS, one, 0)


def prepare(place, route, rlim, clim, psi, near, middle, far):
    part = (BLOCKS, ROWS, WIDTH)
    whole = pl.BlockSpec(part, lambda i, *_: (0, 0, 0))
    return pl.pallas_call(
        prepare_kernel,
        grid_spec=pltpu.PrefetchScalarGridSpec(
            num_scalar_prefetch=4,
            grid=(1,),
            in_specs=[pl.BlockSpec(part, lambda i, place, *_: (0, place[2], 0)), whole, whole, whole],
            out_specs=[whole, whole, whole],
        ),
        out_shape=[
            jax.ShapeDtypeStruct(part, jnp.bfloat16),
            jax.ShapeDtypeStruct(part, jnp.float32),
            jax.ShapeDtypeStruct(part, jnp.bfloat16),
        ],
        compiler_params=pltpu.CompilerParams(vmem_limit_bytes=VMEM),
        cost_estimate=pl.CostEstimate(flops=0, bytes_accessed=20 * 2**20, transcendentals=0),
        name="prepare",
    )(place, route, rlim, clim, psi, near, middle, far)


def residual_kernel(sigma32, amplitude, gathered, out, products):
    line = jnp.sum(gathered[...], axis=0, keepdims=True)
    lane = lax.broadcasted_iota(jnp.int32, (1, 8), 1)

    def pick(n):
        return jnp.sum(jnp.where(lane == n, line, 0.0), axis=1, keepdims=True)

    theta = jnp.broadcast_to(pick(0) / pick(1), (1, WIDTH))
    products[0] = jnp.sum(jnp.where(lane == 2, line, 0.0))
    products[1] = jnp.sum(jnp.where(lane == 3, line, 0.0))

    def one(n, carry):
        for q in range(8):
            b = n * 8 + q
            out[b] = (sigma32[b] - theta * amplitude[b].astype(jnp.float32)).astype(jnp.bfloat16)
        return carry

    lax.fori_loop(0, BLOCKS // 8, one, 0)


def make_residual(sigma32, amplitude, gathered):
    return pl.pallas_call(
        residual_kernel,
        in_specs=[vmem(), vmem(), vmem()],
        out_specs=[vmem(), smem()],
        out_shape=[
            jax.ShapeDtypeStruct((BLOCKS, ROWS, WIDTH), jnp.bfloat16),
            jax.ShapeDtypeStruct((2,), jnp.float32),
        ],
        compiler_params=pltpu.CompilerParams(vmem_limit_bytes=VMEM),
        cost_estimate=NOTHING,
        name="residual",
    )(sigma32, amplitude, gathered)


def halve_kernel(up, down, low, high, buf, sems):
    half = TERMS // 2
    arrive, leave = [], []
    for t in range(half):
        for n, (source, first, target) in enumerate(((up, 0, low), (down, half, high))):
            at = 2 * t + n
            arrive.append(pltpu.make_async_copy(source.at[first + t], buf.at[at], sems.at[0, at]))
            leave.append(pltpu.make_async_copy(buf.at[at], target.at[t], sems.at[1, at]))
    for c in arrive:
        c.start()
    for c, d in zip(arrive, leave):
        c.wait()
        d.start()
    for d in leave:
        d.wait()


def halve(up, down):
    shape = jax.ShapeDtypeStruct((TERMS // 2,) + up.shape[1:], up.dtype)
    return pl.pallas_call(
        halve_kernel,
        in_specs=[anywhere(), anywhere()],
        out_specs=[anywhere(), anywhere()],
        out_shape=[shape, shape],
        scratch_shapes=[
            pltpu.VMEM((TERMS,) + up.shape[1:], up.dtype),
            pltpu.SemaphoreType.DMA((2, TERMS)),
        ],
        compiler_params=pltpu.CompilerParams(vmem_limit_bytes=VMEM),
        cost_estimate=NOTHING,
        name="halve",
    )(up, down)


def after(x, *others):
    return lax.optimization_barrier((x,) + others)[0]


def body(
    wavefunction,
    vectors,
    left_env,
    right_env,
    left_pattern,
    right_pattern,
    block_left,
    block_right,
    left_dims,
    right_dims,
):
    sec = lax.axis_index("sec").astype(jnp.int32)
    op = lax.axis_index("op").astype(jnp.int32)
    place = jnp.stack([sec, (sec // NC) % NZ, op]).astype(jnp.int32)

    right_table = right_env * right_pattern[:, :, None, None].astype(jnp.bfloat16)
    left_env = after(left_env, right_table)
    left_table = left_env * left_pattern[:, :, None, None].astype(jnp.bfloat16)
    rights = {0: (right_table,)}

    def ring(up, down):
        return lax.ppermute(up, "sec", RING_UP), lax.ppermute(down, "sec", RING_DOWN)

    up, down = ring(right_table, right_table)
    left_all = lax.all_gather(left_table, "sec", axis_index_groups=GROUP_XC)
    send, route, rlim, clim = pack(place, block_left, block_right, left_dims, right_dims, wavefunction)
    own = lax.all_to_all(send, "sec", 0, 0, axis_index_groups=GROUP_XC)
    below = lax.ppermute(own, "op", OP_UP)
    above = lax.ppermute(own, "op", OP_DOWN)
    up, down = after(up, own), after(down, own)
    rights[7], rights[1] = (up,), (down,)

    up, down = ring(up, down)
    far_low = lax.ppermute(below[:4], "op", OP_UP)
    far_high = lax.ppermute(above[4:], "op", OP_DOWN)
    up, down = after(up, far_low, far_high), after(down, far_low, far_high)
    rights[6], rights[2] = (up,), (down,)
    pieces = (own, below, above, far_low, far_high)
    heads = [p[:, PIECE : PIECE + 4, 0] for p in (own, above, jnp.concatenate([far_low, far_high]), below)]
    meta = jnp.stack(heads).astype(jnp.int32).reshape(-1)

    up, down = ring(up, down)

    def give_back(coded):
        coded = coded.reshape((NG * NY,) + coded.shape[2:])
        return lax.all_to_all(coded, ("sec", "op"), 0, 0, axis_index_groups=GROUP_XCY)

    near_codes = contract(NEAR, place, meta, pieces, left_all, [rights[d] for d in NEAR])
    rights[5], rights[3] = (up,), (down,)
    up, down = after(up, near_codes), after(down, near_codes)
    low, high = halve(up, down)
    rights[4] = ring(low, high)
    near_back = give_back(near_codes)
    near, sums = decode((NEAR,), place, route, rlim, clim, wavefunction, vectors, near_back)
    middle_codes = contract(MIDDLE, place, meta, pieces, left_all, [rights[d] for d in MIDDLE])
    middle_back = give_back(after(middle_codes, near_back, low, high))
    far_codes = contract(FAR, place, meta, pieces, left_all, [rights[d] for d in FAR])
    middle, sums = decode(
        (MIDDLE,), place, route, rlim, clim, wavefunction, vectors, middle_back, sums
    )
    far_back = give_back(after(far_codes, middle_back))
    far, spread = decode((FAR,), place, route, rlim, clim, wavefunction, vectors, far_back, sums, True)
    gathered = lax.all_to_all(spread, ("sec", "op"), 0, 0, tiled=True)
    sigma16, sigma32, amplitude = prepare(
        place, route, rlim, clim, wavefunction, near, middle, far
    )
    residual, products = make_residual(sigma32, amplitude, gathered)
    return (sigma16, residual, products)


def solution(mesh):
    placed = (
        P("sec", None, None),
        P(None, "sec", None, None),
        P("op", "sec", None, None),
        P("op", "sec", None, None),
        P("op", "sec"),
        P("op", "sec"),
        P("sec"),
        P(),
        P("sec"),
        P(),
    )
    return jax.shard_map(
        body,
        mesh=mesh,
        in_specs=placed,
        out_specs=(P("sec", "op", None), P("sec", "op", None), P()),
        check_vma=False,
    )
```

```python
import jax
import jax.numpy as jnp
from jax import lax
from jax.experimental import pallas as pl
from jax.experimental.pallas import tpu as pltpu
from jax.sharding import PartitionSpec as P

NX, NZ, NC, NY = 4, 8, 2, 4
NG = NX * NC
DEVICES = NX * NZ * NC * NY
BLOCKS, WIDTH, TERMS, SECTORS = 64, 128, 4, 16
ROWS = WIDTH // NY
PIECE = 4 * WIDTH
HEAD = 16
BATCH = 8
DEPTH = 3 * BATCH
CODE_BITS = 13.0
VMEM = 48 * 1024 * 1024
VMEM_ALL = 61 * 1024 * 1024
NOTHING = pl.CostEstimate(flops=1024, bytes_accessed=1024, transcendentals=0)


def sec_index(x, z, c):
    return (x * NZ + z) * NC + c


GROUP_XC = [[sec_index(x, z, c) for x in range(NX) for c in range(NC)] for z in range(NZ)]
GROUP_XCY = [
    [sec_index(x, z, c) * NY + y for x in range(NX) for c in range(NC) for y in range(NY)]
    for z in range(NZ)
]
RING_UP = [
    (sec_index(x, z, c), sec_index(x, (z + 1) % NZ, c))
    for x in range(NX)
    for z in range(NZ)
    for c in range(NC)
]
RING_DOWN = [(d, s) for s, d in RING_UP]
OP_UP = [(y, (y + 1) % NY) for y in range(NY)]
OP_DOWN = [(d, s) for s, d in OP_UP]
NEAR, MIDDLE, FAR = (0, 1, 7, 2, 6), (3, 5), (4,)


def smem():
    return pl.BlockSpec(memory_space=pltpu.SMEM)


def vmem():
    return pl.BlockSpec(memory_space=pltpu.VMEM)


def anywhere():
    return pl.BlockSpec(memory_space=pl.ANY)


def pack_kernel(
    place, block_left, block_right, left_dims, right_dims, psi, send, route, rlim, clim, count, codes
):
    sec = place[0]
    z_here = place[1]
    op = place[2]

    def clear(i, carry):
        count[i] = 0
        return carry

    lax.fori_loop(0, NX * NZ * NC, clear, 0)
    codes[...] = jnp.zeros_like(codes)
    rows = lax.broadcasted_iota(jnp.int32, (WIDTH, WIDTH), 0)
    cols = lax.broadcasted_iota(jnp.int32, (WIDTH, WIDTH), 1)

    def one(b, carry):
        left = block_left[b] - sec * SECTORS
        right = block_right[sec * BLOCKS + b]
        owner = lax.shift_right_logical(right, 4)
        rank = count[owner]
        count[owner] = rank + 1
        x_r = lax.shift_right_logical(owner, 4)
        z_r = lax.shift_right_logical(owner, 1) & 7
        group = x_r * 2 + (owner & 1)
        delta = (z_r - z_here) & 7
        route[b] = group * 16 + delta * 2 + rank
        rl = left_dims[left]
        cl = right_dims[right]
        rlim[b] = rl
        clim[b] = cl

        @pl.when(lax.shift_right_logical(delta, 1) == op)
        def _():
            sub = (delta & 1) * 2 + rank
            block = psi[b].astype(jnp.float32)
            live = (rows < rl) & (cols < cl)
            start = pl.multiple_of(sub * WIDTH, WIDTH)
            send[group, pl.ds(start, WIDTH)] = jnp.where(live, block, 0.0).astype(jnp.bfloat16)
            code = (left * 16 + (right & 15) + 1).astype(jnp.float32)
            codes[group, pl.ds(sub, 1)] = jnp.full((1, WIDTH), 1.0, jnp.float32) * code

        return carry

    lax.fori_loop(0, BLOCKS, one, 0)
    send[:, PIECE:] = codes[...].astype(jnp.bfloat16)


def pack(place, block_left, block_right, left_dims, right_dims, psi):
    return pl.pallas_call(
        pack_kernel,
        in_specs=[smem(), smem(), smem(), smem(), smem(), vmem()],
        out_specs=[vmem(), smem(), smem(), smem()],
        out_shape=[
            jax.ShapeDtypeStruct((NG, PIECE + HEAD, WIDTH), jnp.bfloat16),
            jax.ShapeDtypeStruct((BLOCKS,), jnp.int32),
            jax.ShapeDtypeStruct((BLOCKS,), jnp.int32),
            jax.ShapeDtypeStruct((BLOCKS,), jnp.int32),
        ],
        scratch_shapes=[
            pltpu.SMEM((NX * NZ * NC,), jnp.int32),
            pltpu.VMEM((NG, HEAD, WIDTH), jnp.float32),
        ],
        compiler_params=pltpu.CompilerParams(vmem_limit_bytes=VMEM),
        cost_estimate=NOTHING,
        name="pack",
    )(place, block_left, block_right, left_dims, right_dims, psi)


def contract(deltas, place, meta, acts, pieces, left_all, rights, carried=None):
    slots = len(deltas) * 2
    most = NG * slots
    rows_own = slots * ROWS + HEAD
    rows_out = rows_own + (0 if carried is None else carried.shape[2])
    split = [len(r) for r in rights]

    def kernel(place, meta, acts, own, below, above, far_low, far_high, left, *rest):
        right_refs, rest = rest[: sum(split)], rest[sum(split) :]
        if carried is not None:
            earlier, rest = rest[0], rest[1:]
        out, listed, psi_buf, left_buf, right_buf, heads, sems = rest
        op = place[2]
        heads[...] = jnp.zeros_like(heads)

        count = jnp.int32(0)
        for k, d in enumerate(deltas):
            relative = (d // 2 - op) & 3

            def scan(i, count):
                g = lax.shift_right_logical(i, 1)
                r = i & 1
                sub = (d & 1) * 2 + r
                code = meta[relative * NG * 4 + g * 4 + sub]

                @pl.when(code > 0)
                def _():
                    listed[count] = (
                        (code - 1) + g * 256 + (k * 2 + r) * 2048 + sub * 65536 + relative * 262144
                    )

                return count + (code > 0).astype(jnp.int32)

            count = lax.fori_loop(0, NG * 2, scan, count)

        def fields(entry):
            return (
                lax.shift_right_logical(entry, 4) & 15,
                entry & 15,
                lax.shift_right_logical(entry, 8) & 7,
                lax.shift_right_logical(entry, 11) & 15,
                lax.shift_right_logical(entry, 16) & 3,
                lax.shift_right_logical(entry, 18) & 3,
            )

        def psi_copy(ref, g, sub, at):
            start = pl.multiple_of(sub * WIDTH, WIDTH)
            return pltpu.make_async_copy(ref.at[g, pl.ds(start, WIDTH)], psi_buf.at[at], sems.at[at, 0])

        def left_copy(g, i, at):
            return pltpu.make_async_copy(left.at[g, :, i], left_buf.at[at], sems.at[at, 1])

        def fetch(n):
            i, j, g, s, sub, relative = fields(listed[n])
            at = lax.rem(n, DEPTH)
            left_copy(g, i, at).start()

            @pl.when(relative == 0)
            def _():
                psi_copy(own, g, sub, at).start()

            @pl.when(relative == 1)
            def _():
                psi_copy(above, g, sub, at).start()

            @pl.when(relative == 3)
            def _():
                psi_copy(below, g, sub, at).start()

            @pl.when((relative == 2) & (g < 4))
            def _():
                psi_copy(far_low, g, sub, at).start()

            @pl.when((relative == 2) & (g >= 4))
            def _():
                psi_copy(far_high, g - 4, sub, at).start()

            k = lax.shift_right_logical(s, 1)
            first = 0
            for n_delta, parts in enumerate(split):
                refs = right_refs[first : first + parts]
                first += parts

                @pl.when(k == n_delta)
                def _():
                    share = TERMS // parts
                    for p, ref in enumerate(refs):
                        pltpu.make_async_copy(
                            ref.at[:, j], right_buf.at[at, pl.ds(p * share, share)], sems.at[at, 2 + p]
                        ).start()

        def arrive(at):
            psi_copy(own, 0, 0, at).wait()
            left_copy(0, 0, at).wait()
            share = TERMS // split[0]
            for p in range(split[0]):
                pltpu.make_async_copy(
                    right_refs[p].at[:, 0], right_buf.at[at, pl.ds(p * share, share)], sems.at[at, 2 + p]
                ).wait()

        def begin(n, carry):
            fetch(n)
            return carry

        lax.fori_loop(0, jnp.minimum(count, 2 * BATCH), begin, 0)
        if carried is not None:
            for g in range(NG):
                out[g, :, rows_own:] = earlier[g]

        def step(m, carry):
            for q in range(BATCH):
                n = (m + 2) * BATCH + q

                @pl.when(n < count)
                def _():
                    fetch(n)

            for q in range(BATCH):
                n = m * BATCH + q

                @pl.when(n < count)
                def _():
                    arrive(lax.rem(n, DEPTH))

            results = []
            for q in range(BATCH):
                n = jnp.minimum(m * BATCH + q, count - 1)
                at = lax.rem(n, DEPTH)
                i, j, g, s, sub, relative = fields(listed[n])
                product = lax.dot_general(
                    left_buf[at].reshape(TERMS * WIDTH, WIDTH),
                    psi_buf[at],
                    (((1,), (0,)), ((), ())),
                    preferred_element_type=jnp.float32,
                )
                terms = []
                for a in range(TERMS):
                    act = jnp.full((WIDTH, WIDTH), acts[(g * TERMS + a) * SECTORS + i], jnp.int32)
                    term = jnp.where(act != 0, product[a * WIDTH : (a + 1) * WIDTH], 0.0)
                    terms.append(term.astype(jnp.bfloat16))
                total = None
                for a in range(0, TERMS, 2):
                    lhs = jnp.concatenate([terms[a], terms[a + 1]], axis=1)
                    rhs = jnp.concatenate([right_buf[at, a], right_buf[at, a + 1]], axis=1)
                    part = lax.dot_general(
                        lhs, rhs, (((1,), (1,)), ((), ())), preferred_element_type=jnp.float32
                    )
                    total = part if total is None else total + part
                peak = jnp.max(jnp.max(jnp.abs(total), axis=0, keepdims=True), axis=1, keepdims=True)
                exponent = jnp.clip(jnp.floor(jnp.log2(peak)), -100.0, 127.0)
                code = jnp.round(total * jnp.exp2(CODE_BITS - exponent)).astype(jnp.int32).astype(jnp.int16)
                results.append((g, s, code, exponent))
            for g, s, code, exponent in results:
                start = pl.multiple_of(s * ROWS, ROWS)
                for y in range(NY):
                    out[g, y, pl.ds(start, ROWS)] = code[y * ROWS : (y + 1) * ROWS]
                heads[g, pl.ds(s, 1)] = jnp.broadcast_to(exponent, (1, WIDTH)).astype(jnp.int32)
            return carry

        lax.fori_loop(0, (count + BATCH - 1) // BATCH, step, 0)
        for y in range(NY):
            out[:, y, slots * ROWS : rows_own] = heads[...].astype(jnp.int16)

    flat = [part for r in rights for part in r]
    return pl.pallas_call(
        kernel,
        in_specs=[smem(), smem(), smem()]
        + [anywhere()] * (len(pieces) + 1 + len(flat))
        + ([] if carried is None else [vmem()]),
        out_specs=vmem(),
        out_shape=jax.ShapeDtypeStruct((NG, NY, rows_out, WIDTH), jnp.int16),
        scratch_shapes=[
            pltpu.SMEM((most,), jnp.int32),
            pltpu.VMEM((DEPTH, WIDTH, WIDTH), jnp.bfloat16),
            pltpu.VMEM((DEPTH, TERMS, WIDTH, WIDTH), jnp.bfloat16),
            pltpu.VMEM((DEPTH, TERMS, WIDTH, WIDTH), jnp.bfloat16),
            pltpu.VMEM((NG, HEAD, WIDTH), jnp.int32),
            pltpu.SemaphoreType.DMA((DEPTH, 4)),
        ],
        compiler_params=pltpu.CompilerParams(vmem_limit_bytes=VMEM_ALL),
        cost_estimate=pl.CostEstimate(
            flops=most * 16 * TERMS * 2 * WIDTH**3, bytes_accessed=most * 2**20, transcendentals=0
        ),
        name="contract",
    )(place, meta, acts, *pieces, left_all, *flat, *([] if carried is None else [carried]))


def first_rows(chunks):
    origins = [0]
    for deltas in chunks:
        origins.append(origins[-1] + len(deltas) * 2 * ROWS + HEAD)
    return origins


def decode_kernel(chunks, later, place, route, rlim, clim, psi, vectors, *rest):
    returned, rest = rest[0], rest[1:]
    before, rest = (rest[0], rest[1:]) if later else (None, rest)
    (sigma32, result), scales = rest[:2], rest[2:]
    first_row = place[2] * ROWS
    rows = lax.broadcasted_iota(jnp.int32, (ROWS, WIDTH), 0) + first_row
    cols = lax.broadcasted_iota(jnp.int32, (ROWS, WIDTH), 1)
    origins = first_rows(chunks)
    for n, deltas in enumerate(chunks):
        top = origins[n] + len(deltas) * 2 * ROWS
        head = returned[:, top : top + HEAD].astype(jnp.int32).astype(jnp.float32)
        scales[n][...] = jnp.exp2(head - CODE_BITS)
    if later:
        result[...] = before[...]
    else:
        result[...] = jnp.zeros_like(result)

    def one(b, carry):
        slot = route[b]
        group = lax.shift_right_logical(slot, 4)
        delta = lax.shift_right_logical(slot, 1) & 7
        rank = slot & 1
        live = (rows < rlim[b]) & (cols < clim[b])
        amp = jnp.where(live, psi[b].astype(jnp.float32), 0.0)
        if not later:
            result[1] += amp * amp
        for n, deltas in enumerate(chunks):
            here = delta == deltas[0]
            place_in = jnp.int32(0)
            for k, d in enumerate(deltas[1:]):
                here = here | (delta == d)
                place_in = jnp.where(delta == d, k + 1, place_in)

            @pl.when(here)
            def _():
                s = place_in * 2 + rank
                start = pl.multiple_of(origins[n] + s * ROWS, HEAD)
                total = None
                for y in range(NY):
                    code = returned[group * NY + y, pl.ds(start, ROWS)]
                    part = code.astype(jnp.int32).astype(jnp.float32) * scales[n][group * NY + y, pl.ds(s, 1)]
                    total = part if total is None else total + part
                value = jnp.where(live, total, 0.0)
                sigma32[b] = value
                result[0] += amp * value
                result[2] += vectors[0, b].astype(jnp.float32) * value
                result[3] += vectors[1, b].astype(jnp.float32) * value

        return carry

    lax.fori_loop(0, BLOCKS, one, 0)


def spread_kernel(sums, spread):
    lane = lax.broadcasted_iota(jnp.int32, (1, WIDTH), 1)
    line = jnp.zeros((1, WIDTH), jnp.float32)
    for n in range(4):
        column = jnp.sum(sums[n], axis=0, keepdims=True)
        line = jnp.where(lane == n, jnp.sum(column, axis=1, keepdims=True), line)
    spread[...] = jnp.broadcast_to(line[:, :8], (DEVICES, 8))


def decode(chunks, place, route, rlim, clim, psi, vectors, returned, before=None, last=False):
    def whole(shape):
        return pl.BlockSpec(shape, lambda i, *_: (0,) * len(shape))

    part = (BLOCKS, ROWS, WIDTH)
    later = before is not None
    sums = (4, ROWS, WIDTH)

    def kernel(*refs):
        if not last:
            decode_kernel(chunks, later, *refs)
            return
        tail = len(chunks) + 1
        decode_kernel(chunks, later, *refs[: -tail - 1], refs[-1], *refs[-tail:-1])
        spread_kernel(refs[-1], refs[-tail - 1])

    return pl.pallas_call(
        kernel,
        grid_spec=pltpu.PrefetchScalarGridSpec(
            num_scalar_prefetch=4,
            grid=(1,),
            in_specs=[
                pl.BlockSpec(part, lambda i, place, *_: (0, place[2], 0)),
                pl.BlockSpec((2,) + part, lambda i, place, *_: (0, 0, place[2], 0)),
            ]
            + [whole(returned.shape)]
            + ([whole(sums)] if later else []),
            out_specs=[whole(part), whole((DEVICES, 8)) if last else whole(sums)],
            scratch_shapes=[pltpu.VMEM((NG * NY, HEAD, WIDTH), jnp.float32) for _ in chunks]
            + ([pltpu.VMEM(sums, jnp.float32)] if last else []),
        ),
        out_shape=[
            jax.ShapeDtypeStruct(part, jnp.float32),
            jax.ShapeDtypeStruct((DEVICES, 8) if last else sums, jnp.float32),
        ],
        compiler_params=pltpu.CompilerParams(vmem_limit_bytes=VMEM),
        cost_estimate=NOTHING,
        name="decode_last" if last else "decode",
    )(place, route, rlim, clim, psi, vectors, returned, *([before] if later else []))


def prepare_kernel(place, route, rlim, clim, psi, near, middle, far, sigma16, sigma32, amplitude):
    first_row = place[2] * ROWS
    rows = lax.broadcasted_iota(jnp.int32, (ROWS, WIDTH), 0) + first_row
    cols = lax.broadcasted_iota(jnp.int32, (ROWS, WIDTH), 1)

    def one(b, carry):
        delta = lax.shift_right_logical(route[b], 1) & 7
        in_middle = (delta == MIDDLE[0]) | (delta == MIDDLE[1])
        in_far = delta == FAR[0]
        live = (rows < rlim[b]) & (cols < clim[b])
        amplitude[b] = jnp.where(live, psi[b].astype(jnp.float32), 0.0).astype(jnp.bfloat16)

        def emit(value):
            sigma32[b] = value
            sigma16[b] = value.astype(jnp.bfloat16)

        @pl.when(in_far)
        def _():
            emit(far[b])

        @pl.when(in_middle)
        def _():
            emit(middle[b])

        @pl.when(jnp.logical_not(in_far | in_middle))
        def _():
            emit(near[b])

        return carry

    lax.fori_loop(0, BLOCKS, one, 0)


def prepare(place, route, rlim, clim, psi, near, middle, far):
    part = (BLOCKS, ROWS, WIDTH)
    whole = pl.BlockSpec(part, lambda i, *_: (0, 0, 0))
    return pl.pallas_call(
        prepare_kernel,
        grid_spec=pltpu.PrefetchScalarGridSpec(
            num_scalar_prefetch=4,
            grid=(1,),
            in_specs=[pl.BlockSpec(part, lambda i, place, *_: (0, place[2], 0)), whole, whole, whole],
            out_specs=[whole, whole, whole],
        ),
        out_shape=[
            jax.ShapeDtypeStruct(part, jnp.bfloat16),
            jax.ShapeDtypeStruct(part, jnp.float32),
            jax.ShapeDtypeStruct(part, jnp.bfloat16),
        ],
        compiler_params=pltpu.CompilerParams(vmem_limit_bytes=VMEM),
        cost_estimate=pl.CostEstimate(flops=0, bytes_accessed=20 * 2**20, transcendentals=0),
        name="prepare",
    )(place, route, rlim, clim, psi, near, middle, far)


def residual_kernel(sigma32, amplitude, gathered, out, products):
    line = jnp.sum(gathered[...], axis=0, keepdims=True)
    lane = lax.broadcasted_iota(jnp.int32, (1, 8), 1)

    def pick(n):
        return jnp.sum(jnp.where(lane == n, line, 0.0), axis=1, keepdims=True)

    theta = jnp.broadcast_to(pick(0) / pick(1), (1, WIDTH))
    products[0] = jnp.sum(jnp.where(lane == 2, line, 0.0))
    products[1] = jnp.sum(jnp.where(lane == 3, line, 0.0))

    def one(n, carry):
        for q in range(8):
            b = n * 8 + q
            out[b] = (sigma32[b] - theta * amplitude[b].astype(jnp.float32)).astype(jnp.bfloat16)
        return carry

    lax.fori_loop(0, BLOCKS // 8, one, 0)


def make_residual(sigma32, amplitude, gathered):
    return pl.pallas_call(
        residual_kernel,
        in_specs=[vmem(), vmem(), vmem()],
        out_specs=[vmem(), smem()],
        out_shape=[
            jax.ShapeDtypeStruct((BLOCKS, ROWS, WIDTH), jnp.bfloat16),
            jax.ShapeDtypeStruct((2,), jnp.float32),
        ],
        compiler_params=pltpu.CompilerParams(vmem_limit_bytes=VMEM),
        cost_estimate=NOTHING,
        name="residual",
    )(sigma32, amplitude, gathered)


def halve_kernel(up, down, low, high, buf, sems):
    half = TERMS // 2
    arrive, leave = [], []
    for t in range(half):
        for n, (source, first, target) in enumerate(((up, 0, low), (down, half, high))):
            at = 2 * t + n
            arrive.append(pltpu.make_async_copy(source.at[first + t], buf.at[at], sems.at[0, at]))
            leave.append(pltpu.make_async_copy(buf.at[at], target.at[t], sems.at[1, at]))
    for c in arrive:
        c.start()
    for c, d in zip(arrive, leave):
        c.wait()
        d.start()
    for d in leave:
        d.wait()


def halve(up, down):
    shape = jax.ShapeDtypeStruct((TERMS // 2,) + up.shape[1:], up.dtype)
    return pl.pallas_call(
        halve_kernel,
        in_specs=[anywhere(), anywhere()],
        out_specs=[anywhere(), anywhere()],
        out_shape=[shape, shape],
        scratch_shapes=[
            pltpu.VMEM((TERMS,) + up.shape[1:], up.dtype),
            pltpu.SemaphoreType.DMA((2, TERMS)),
        ],
        compiler_params=pltpu.CompilerParams(vmem_limit_bytes=VMEM),
        cost_estimate=NOTHING,
        name="halve",
    )(up, down)


def after(x, *others):
    return lax.optimization_barrier((x,) + others)[0]


def body(
    wavefunction,
    vectors,
    left_env,
    right_env,
    left_pattern,
    right_pattern,
    block_left,
    block_right,
    left_dims,
    right_dims,
):
    sec = lax.axis_index("sec").astype(jnp.int32)
    op = lax.axis_index("op").astype(jnp.int32)
    place = jnp.stack([sec, (sec // NC) % NZ, op]).astype(jnp.int32)

    right_table = right_env * right_pattern[:, :, None, None].astype(jnp.bfloat16)
    rights = {0: (right_table,)}

    def ring(up, down):
        return lax.ppermute(up, "sec", RING_UP), lax.ppermute(down, "sec", RING_DOWN)

    up, down = ring(right_table, right_table)
    left_all = lax.all_gather(left_env, "sec", axis_index_groups=GROUP_XC)
    send, route, rlim, clim = pack(place, block_left, block_right, left_dims, right_dims, wavefunction)
    own = lax.all_to_all(send, "sec", 0, 0, axis_index_groups=GROUP_XC)
    below = lax.ppermute(own, "op", OP_UP)
    above = lax.ppermute(own, "op", OP_DOWN)
    acts = jnp.broadcast_to(after(left_pattern, own)[None], (NG,) + left_pattern.shape)
    acts = lax.all_to_all(acts, "sec", 0, 0, axis_index_groups=GROUP_XC).reshape(-1)
    up, down = after(up, own, acts), after(down, own, acts)
    rights[7], rights[1] = (up,), (down,)

    up, down = ring(up, down)
    far_low = lax.ppermute(below[:4], "op", OP_UP)
    far_high = lax.ppermute(above[4:], "op", OP_DOWN)
    up, down = after(up, far_low, far_high), after(down, far_low, far_high)
    rights[6], rights[2] = (up,), (down,)
    pieces = (own, below, above, far_low, far_high)
    heads = [p[:, PIECE : PIECE + 4, 0] for p in (own, above, jnp.concatenate([far_low, far_high]), below)]
    meta = jnp.stack(heads).astype(jnp.int32).reshape(-1)

    up, down = ring(up, down)

    def give_back(coded):
        coded = coded.reshape((NG * NY,) + coded.shape[2:])
        return lax.all_to_all(coded, ("sec", "op"), 0, 0, axis_index_groups=GROUP_XCY)

    near_codes = contract(NEAR, place, meta, acts, pieces, left_all, [rights[d] for d in NEAR])
    rights[5], rights[3] = (up,), (down,)
    up, down = after(up, near_codes), after(down, near_codes)
    low, high = halve(up, down)
    rights[4] = ring(low, high)
    near_back = give_back(near_codes)
    near, sums = decode((NEAR,), place, route, rlim, clim, wavefunction, vectors, near_back)
    middle_codes = contract(MIDDLE, place, meta, acts, pieces, left_all, [rights[d] for d in MIDDLE])
    middle_back = give_back(after(middle_codes, near_back, low, high))
    far_codes = contract(FAR, place, meta, acts, pieces, left_all, [rights[d] for d in FAR])
    middle, sums = decode(
        (MIDDLE,), place, route, rlim, clim, wavefunction, vectors, middle_back, sums
    )
    far_back = give_back(after(far_codes, middle_back))
    far, spread = decode((FAR,), place, route, rlim, clim, wavefunction, vectors, far_back, sums, True)
    gathered = lax.all_to_all(spread, ("sec", "op"), 0, 0, tiled=True)
    sigma16, sigma32, amplitude = prepare(
        place, route, rlim, clim, wavefunction, near, middle, far
    )
    residual, products = make_residual(sigma32, amplitude, gathered)
    return (sigma16, residual, products)


def solution(mesh):
    placed = (
        P("sec", None, None),
        P(None, "sec", None, None),
        P("op", "sec", None, None),
        P("op", "sec", None, None),
        P("op", "sec"),
        P("op", "sec"),
        P("sec"),
        P(),
        P("sec"),
        P(),
    )
    return jax.shard_map(
        body,
        mesh=mesh,
        in_specs=placed,
        out_specs=(P("sec", "op", None), P("sec", "op", None), P()),
        check_vma=False,
    )
```
